32 devices in a mesh: tm: 4 (over y, x), rows: 8 (over z, core).
Axes of the slice: x: 2, y: 2, z: 4, core: 2. Of those that a mesh axis runs over, the one named last changes fastest.
Arguments:
- latent: bfloat16 [4, 8, 160, 512], P('tm', 'rows'), may hold values from -350 to 350, as said below
- norm_gain: float32 [512], replicated, may hold values from 0.1 to 1.9
- norm_bias: float32 [512], replicated, may hold values from -4 to 4
- conv_weight: bfloat16 [3, 3, 3, 512, 512], P(None, None, None, 'rows', 'tm'), may hold values from -0.0546875 to 0.0546875
- cotangent: bfloat16 [4, 16, 320, 512], P('tm', 'rows'), may hold values from -180 to 180
Outputs:
- latent_grad: float32 [4, 8, 160, 512], P('tm', 'rows')
- gain_grad: float32 [512], replicated
- bias_grad: float32 [512], replicated
The draws below stay inside these ranges and needn't reach their ends.
Inputs may be any that keep to these rules, and one draw needn't show every extreme that they name: `latent`: features of the unit's input.
All inputs are finite; a program needn't handle non-finite values.
Results may differ from the reference program's by a relative error of at most 0.0003.
Values may be sent and summed in bfloat16 or wider, within the bound.
A program may use at most 320 MiB of HBM per device.

```python
import math
import jax
import jax.numpy as jnp
from jax import lax

CH = 512
GROUPS = 32
COLS = 160
FRAMES = 4
LROWS = 8


def rising(count, factor):
    position = jnp.arange(count, dtype=jnp.float32) / max(count - 1, 1)
    return jnp.power(factor, position)


def draw_latent(key, part):
    key_parts = jax.random.split(key, 3)
    chan_scale = jnp.exp(jax.random.uniform(key_parts[0], (CH,), jnp.float32, math.log(0.5), math.log(5.0)))
    chan_offset = jax.random.uniform(key_parts[1], (CH,), jnp.float32, -1.0, 1.0)
    shape = (FRAMES, LROWS, COLS, CH)
    random_part = jnp.clip(jax.random.normal(key_parts[2], shape, jnp.float32), -4.0, 4.0)
    row_rise = rising(LROWS, 3.0)
    frame_rise = rising(FRAMES, 1.5)
    values = (random_part + chan_offset) * chan_scale * row_rise[None, :, None, None] * frame_rise[:, None, None, None]
    return values.astype(jnp.bfloat16)


def draw_cotangent(key, part):
    key_parts = jax.random.split(key, 3)
    chan_scale = jnp.exp(jax.random.uniform(key_parts[0], (CH,), jnp.float32, math.log(0.4), math.log(4.0)))
    chan_offset = jax.random.uniform(key_parts[1], (CH,), jnp.float32, -0.7, 0.7)
    shape = (FRAMES, 2 * LROWS, 2 * COLS, CH)
    random_part = jnp.clip(jax.random.normal(key_parts[2], shape, jnp.float32), -4.0, 4.0)
    row_rise = rising(2 * LROWS, 3.0)
    values = (random_part + chan_offset) * chan_scale * row_rise[None, :, None, None]
    return values.astype(jnp.bfloat16)


def level_of(key, shape, pieces, low, largest):
    def one(dim, shards_of):
        draws = jax.random.uniform(jax.random.fold_in(jax.random.fold_in(key, 6), dim), (shards_of,), jnp.float32, low / len(pieces), largest / len(pieces))
        return jnp.repeat(jnp.exp(draws), shape[dim] // shards_of).reshape((-1,) + (1,) * (len(shape) - dim - 1))

    gain = one(*pieces[0])
    for cut in pieces[1:]:
        gain = gain * one(*cut)
    return gain


def bell_draw(stream_key, extent, scale, bound, shards=(), held_as=jnp.bfloat16):
    level = level_of(stream_key, extent, shards, -0.22, 0.18) if shards else 1.0
    values = jax.random.normal(stream_key, extent, jnp.float32) * scale * level
    return jnp.minimum(jnp.maximum(values, -bound), bound).astype(held_as)


def setup_inputs(seed: int = 0) -> dict:
    key_list = jax.random.split(jax.random.key(seed), 6)
    latent = draw_latent(jax.random.fold_in(key_list[5], 71), 0)
    norm_gain = jnp.clip(1.0 + 0.18 * jax.random.normal(key_list[1], (CH,), jnp.float32), 0.1, 1.9)
    norm_bias = bell_draw(key_list[2], (CH,), 1.0, 4.0, (), jnp.float32)
    conv_weight = bell_draw(key_list[3], (3, 3, 3, CH, CH), (27 * CH) ** -0.5, 0.0546875, ((3, 8), (4, 4)))
    cotangent = draw_cotangent(jax.random.fold_in(key_list[5], 71), 0)
    return dict(latent=latent, norm_gain=norm_gain, norm_bias=norm_bias, conv_weight=conv_weight, cotangent=cotangent)


def tap_total(row_slabs, conv_weight, tap_pairs, frames_out, span_cols):
    running = None
    for offset, tap_index in tap_pairs:
        for row_tap in range(3):
            source = row_slabs[row_tap][offset:offset + frames_out].astype(jnp.float32)
            for col_tap in range(3):
                kernel = conv_weight[tap_index, row_tap, col_tap].astype(jnp.float32)
                product = lax.dot_general(source, kernel, (((3,), (1,)), ((), ())), precision=lax.Precision.HIGHEST, preferred_element_type=jnp.float32)
                piece = product[:, :, 2 - col_tap:2 - col_tap + span_cols, :]
                running = piece if running is None else running + piece
    return running

def pool_pairs(fine_grad):
    frames, fine_rows, span_cols, channels = fine_grad.shape
    return fine_grad.reshape(frames, fine_rows // 2, 2, span_cols // 2, 2, channels).sum(axis=(2, 4))

def reference(latent, norm_gain, norm_bias, conv_weight, cotangent):
    frames = cotangent.shape[0]
    fine_rows = cotangent.shape[1]
    span_cols = cotangent.shape[2]
    padded = jnp.pad(cotangent, ((0, 2), (1, 1), (1, 1), (0, 0)))
    row_slabs = [padded[:, 2 - row_tap:2 - row_tap + fine_rows] for row_tap in range(3)]
    main_part = tap_total(row_slabs, conv_weight, ((0, 2), (1, 1), (2, 0)), frames, span_cols)
    extra_part = tap_total(row_slabs, conv_weight, ((0, 1), (0, 0), (1, 0)), 1, span_cols)
    fine_grad = jnp.concatenate([main_part[:1] + extra_part, main_part[1:]], axis=0)
    up_grad = pool_pairs(fine_grad)
    channels = latent.shape[3]
    per_group = channels // GROUPS
    cell_count = latent.shape[0] * latent.shape[1] * latent.shape[2]
    features = latent.astype(jnp.float32)
    sum_x = lax.optimization_barrier(jnp.sum(features, axis=(0, 1, 2))).reshape(GROUPS, per_group).sum(axis=1)
    sum_sq = lax.optimization_barrier(jnp.sum(features * features, axis=(0, 1, 2))).reshape(GROUPS, per_group).sum(axis=1)
    group_mean = sum_x / (cell_count * per_group)
    group_var = sum_sq / (cell_count * per_group) - group_mean * group_mean
    inv_std = lax.rsqrt(group_var + 1e-06)
    mean_chan = jnp.repeat(group_mean, per_group)
    inv_chan = jnp.repeat(inv_std, per_group)
    normed = (features - mean_chan) * inv_chan
    pre = normed * norm_gain + norm_bias
    sigmoid_pre = jax.nn.sigmoid(pre)
    act_grad = up_grad * sigmoid_pre * (1.0 + pre * (1.0 - sigmoid_pre))
    sum_act = lax.optimization_barrier(jnp.sum(act_grad, axis=(0, 1, 2)))
    sum_scaled = lax.optimization_barrier(jnp.sum(act_grad * normed, axis=(0, 1, 2)))
    gain_grad = sum_scaled / cell_count
    bias_grad = sum_act / cell_count
    mean_q = (norm_gain * sum_act).reshape(GROUPS, per_group).sum(axis=1) / (cell_count * per_group)
    mean_qn = (norm_gain * sum_scaled).reshape(GROUPS, per_group).sum(axis=1) / (cell_count * per_group)
    latent_grad = inv_chan * (act_grad * norm_gain - jnp.repeat(mean_q, per_group) - normed * jnp.repeat(mean_qn, per_group))
    return (latent_grad, gain_grad, bias_grad)
```

```python
import jax
import jax.numpy as jnp
from jax import lax
from jax.sharding import PartitionSpec as P

GROUPS = 32


def split_pair(value):
    high = lax.reduce_precision(value, 8, 7)
    return high.astype(jnp.bfloat16), (value - high).astype(jnp.bfloat16)


def row_rims(block):
    count = lax.axis_size("rows")
    forward = [(i, i + 1) for i in range(count - 1)]
    backward = [(target, source) for source, target in forward]
    low = lax.ppermute(block[:, -1:], "rows", forward)
    high = lax.ppermute(block[:, :1], "rows", backward)
    return jnp.concatenate([low, block, high], axis=1)


def box_sums(block):
    wide = jnp.pad(block.astype(jnp.float32), ((0, 0), (0, 0), (1, 1), (0, 0)))
    rows = wide[:, :-1] + wide[:, 1:]
    return rows[:, :, :-1] + rows[:, :, 1:]


def up_grad_part(boxes, weights, low_rows, low_cols):
    frames = boxes.shape[0]
    early = [boxes[:1]]
    for t in (1, 2):
        early.append(early[-1] + boxes[t : t + 1])
    total = None
    for a in range(3):
        stack = jnp.concatenate([early[2 - a], boxes[3 - a :]], axis=0)
        taps = []
        for b in range(3):
            for c in range(3):
                taps.append(
                    stack[:, 2 - b : 1 - b + 2 * low_rows : 2, 2 - c : 1 - c + 2 * low_cols : 2]
                )
        wide = jnp.concatenate(taps, axis=-1)
        kernel = jnp.concatenate([weights[a, b, c] for b in range(3) for c in range(3)], axis=-1)
        high, low = split_pair(wide)
        product = sum(
            lax.dot_general(
                part, kernel, (((3,), (1,)), ((), ())), preferred_element_type=jnp.float32
            )
            for part in (high, low)
        )
        product = jnp.pad(product, ((0, frames - product.shape[0]), (0, 0), (0, 0), (0, 0)))
        total = product if total is None else total + product
    return total


def spread_out(latent, norm_gain, norm_bias, conv_weight, cotangent):
    frames_all = lax.axis_size("tm")
    rows_all = lax.axis_size("rows")
    low_rows, low_cols, channels = latent.shape[1:]
    per_group = channels // GROUPS
    cell_count = frames_all * rows_all * low_rows * low_cols
    weights = lax.all_gather(conv_weight, "rows", axis=3, tiled=True)
    swapped = lax.all_to_all(cotangent, "tm", split_axis=3, concat_axis=0, tiled=True)
    part = up_grad_part(box_sums(row_rims(swapped)), weights, low_rows, low_cols)
    up_grad = lax.psum_scatter(part, "tm", scatter_dimension=0, tiled=True)
    features = latent.astype(jnp.float32)
    sum_x = jnp.sum(features, axis=(0, 1, 2))
    sum_sq = jnp.sum(features * features, axis=(0, 1, 2))
    total_x, total_sq = lax.psum((sum_x, sum_sq), ("tm", "rows"))
    group_x = total_x.reshape(GROUPS, per_group).sum(axis=1)
    group_sq = total_sq.reshape(GROUPS, per_group).sum(axis=1)
    group_mean = group_x / (cell_count * per_group)
    group_var = group_sq / (cell_count * per_group) - group_mean * group_mean
    inv_std = lax.rsqrt(group_var + 1e-06)
    mean_chan = jnp.repeat(group_mean, per_group)
    inv_chan = jnp.repeat(inv_std, per_group)
    normed = (features - mean_chan) * inv_chan
    pre = normed * norm_gain + norm_bias
    sigmoid_pre = jax.nn.sigmoid(pre)
    act_grad = up_grad * sigmoid_pre * (1.0 + pre * (1.0 - sigmoid_pre))
    sum_act, sum_scaled = lax.psum(
        (jnp.sum(act_grad, axis=(0, 1, 2)), jnp.sum(act_grad * normed, axis=(0, 1, 2))),
        ("tm", "rows"),
    )
    gain_grad = sum_scaled / cell_count
    bias_grad = sum_act / cell_count
    mean_q = (norm_gain * sum_act).reshape(GROUPS, per_group).sum(axis=1) / (cell_count * per_group)
    mean_qn = (norm_gain * sum_scaled).reshape(GROUPS, per_group).sum(axis=1) / (
        cell_count * per_group
    )
    latent_grad = inv_chan * (
        act_grad * norm_gain
        - jnp.repeat(mean_q, per_group)
        - normed * jnp.repeat(mean_qn, per_group)
    )
    return (latent_grad, gain_grad, bias_grad)


def solution(mesh):
    placed = (
        P("tm", "rows", None, None),
        P(),
        P(),
        P(None, None, None, "rows", "tm"),
        P("tm", "rows", None, None),
    )
    return jax.shard_map(
        spread_out,
        mesh=mesh,
        in_specs=placed,
        out_specs=(P("tm", "rows", None, None), P(), P()),
        check_vma=False,
    )
```

```python
import functools

import jax
import jax.numpy as jnp
from jax import lax
from jax.experimental import pallas as pl
from jax.experimental.pallas import tpu as pltpu
from jax.sharding import PartitionSpec as P

GROUPS = 32


def split_pair(value):
    high = lax.reduce_precision(value, 8, 7)
    return high.astype(jnp.bfloat16), (value - high).astype(jnp.bfloat16)


def row_rims(block):
    count = lax.axis_size("rows")
    forward = [(i, i + 1) for i in range(count - 1)]
    backward = [(target, source) for source, target in forward]
    low = lax.ppermute(block[:, -1:], "rows", forward)
    high = lax.ppermute(block[:, :1], "rows", backward)
    return jnp.concatenate([low, block, high], axis=1)


def box_sums(block):
    wide = jnp.pad(block.astype(jnp.float32), ((0, 0), (0, 0), (1, 1), (0, 0)))
    rows = wide[:, :-1] + wide[:, 1:]
    return rows[:, :, :-1] + rows[:, :, 1:]


def up_grad_part(boxes, weights, low_rows, low_cols):
    frames = boxes.shape[0]
    early = [boxes[:1]]
    for t in (1, 2):
        early.append(early[-1] + boxes[t : t + 1])
    total = None
    for a in range(3):
        stack = jnp.concatenate([early[2 - a], boxes[3 - a :]], axis=0)
        taps = []
        for b in range(3):
            for c in range(3):
                taps.append(
                    stack[:, 2 - b : 1 - b + 2 * low_rows : 2, 2 - c : 1 - c + 2 * low_cols : 2]
                )
        wide = jnp.concatenate(taps, axis=-1)
        kernel = jnp.concatenate([weights[a, b, c] for b in range(3) for c in range(3)], axis=-1)
        high, low = split_pair(wide)
        product = sum(
            lax.dot_general(
                part, kernel, (((3,), (1,)), ((), ())), preferred_element_type=jnp.float32
            )
            for part in (high, low)
        )
        product = jnp.pad(product, ((0, frames - product.shape[0]), (0, 0), (0, 0), (0, 0)))
        total = product if total is None else total + product
    return total


def spread_out(latent, norm_gain, norm_bias, conv_weight, cotangent):
    frames_all = lax.axis_size("tm")
    rows_all = lax.axis_size("rows")
    low_rows, low_cols, channels = latent.shape[1:]
    per_group = channels // GROUPS
    cell_count = frames_all * rows_all * low_rows * low_cols
    weights = lax.all_gather(conv_weight, "rows", axis=3, tiled=True)
    swapped = lax.all_to_all(cotangent, "tm", split_axis=3, concat_axis=0, tiled=True)
    part = up_grad_part(box_sums(row_rims(swapped)), weights, low_rows, low_cols)
    up_grad = lax.psum_scatter(part, "tm", scatter_dimension=0, tiled=True)
    features = latent.astype(jnp.float32)
    sum_x = jnp.sum(features, axis=(0, 1, 2))
    sum_sq = jnp.sum(features * features, axis=(0, 1, 2))
    total_x, total_sq = lax.psum((sum_x, sum_sq), ("tm", "rows"))
    group_x = total_x.reshape(GROUPS, per_group).sum(axis=1)
    group_sq = total_sq.reshape(GROUPS, per_group).sum(axis=1)
    group_mean = group_x / (cell_count * per_group)
    group_var = group_sq / (cell_count * per_group) - group_mean * group_mean
    inv_std = lax.rsqrt(group_var + 1e-06)
    mean_chan = jnp.repeat(group_mean, per_group)
    inv_chan = jnp.repeat(inv_std, per_group)
    normed = (features - mean_chan) * inv_chan
    pre = normed * norm_gain + norm_bias
    sigmoid_pre = jax.nn.sigmoid(pre)
    act_grad = up_grad * sigmoid_pre * (1.0 + pre * (1.0 - sigmoid_pre))
    sum_act, sum_scaled = lax.psum(
        (jnp.sum(act_grad, axis=(0, 1, 2)), jnp.sum(act_grad * normed, axis=(0, 1, 2))),
        ("tm", "rows"),
    )
    gain_grad = sum_scaled / cell_count
    bias_grad = sum_act / cell_count
    mean_q = (norm_gain * sum_act).reshape(GROUPS, per_group).sum(axis=1) / (cell_count * per_group)
    mean_qn = (norm_gain * sum_scaled).reshape(GROUPS, per_group).sum(axis=1) / (
        cell_count * per_group
    )
    latent_grad = inv_chan * (
        act_grad * norm_gain
        - jnp.repeat(mean_q, per_group)
        - normed * jnp.repeat(mean_qn, per_group)
    )
    return (latent_grad, gain_grad, bias_grad)


MESH = pl.DeviceIdType.MESH


def group_totals(value, member):
    first = value.astype(jnp.bfloat16).astype(jnp.float32)
    rest = value - first
    second = rest.astype(jnp.bfloat16).astype(jnp.float32)
    third = rest - second
    parts = jnp.concatenate([first, second, third, jnp.zeros_like(first)], axis=0)
    sums = jnp.dot(parts.astype(jnp.bfloat16), member, preferred_element_type=jnp.float32)
    rows = value.shape[0]
    return sums[:rows] + sums[rows : 2 * rows] + sums[2 * rows : 3 * rows]


def fused_kernel(
    frames, count, per_group, cells,
    ct, w, lat, gain, bias,
    out, gain_out, bias_out,
    fine, wbuf, wcat, stack, pad, part, inbox, normed, slope, chan, member, st_rows, st_tm,
    local_sem, ct_send, ct_recv, rim_send, rim_recv, z_send, z_recv, sib_send, sib_recv,
    part_send, part_recv, sr_send, sr_recv, st_send, st_recv,
):
    chips = count // 2
    low_cols, channels = lat.shape
    fine_cols = ct.shape[1]
    width = w.shape[2]
    half = w.shape[1]
    me_t = lax.axis_index("tm")
    me_r = lax.axis_index("rows")
    z = lax.div(me_r, 2)
    core = lax.rem(me_r, 2)
    sibling = me_r + 1 - 2 * core

    def remote(src, dst, send, recv, t, r):
        return pltpu.make_async_remote_copy(
            src_ref=src, dst_ref=dst, send_sem=send, recv_sem=recv,
            device_id=(t, r), device_id_type=MESH,
        )

    def frame_at(d):
        return lax.rem(me_t + d, frames)

    def row_at(d):
        return lax.rem(me_r + d, count)

    def lanes(t):
        return pl.ds(pl.multiple_of(t * width, width), width)

    def ct_copy(d):
        t = frame_at(d)
        return remote(
            ct.at[:, :, lanes(t)], fine.at[me_t, pl.ds(1, 2)],
            ct_send.at[d - 1], ct_recv.at[d - 1], t, me_r,
        )

    def rim_copy(side):
        return remote(
            fine.at[:, 1 + side], fine.at[:, 3 - 3 * side],
            rim_send.at[side], rim_recv.at[side], me_t, row_at(count - 1 + 2 * side),
        )

    def z_copy(side, step, chip, first):
        src = w if first else wbuf.at[chip, core]
        to = row_at(2 if side == 0 else count - 2)
        return remote(
            src, wbuf.at[chip, core], z_send.at[side, step - 1], z_recv.at[side, step - 1],
            me_t, to,
        )

    def sib_copy(chip, first):
        src = w if first else wbuf.at[chip, core]
        return remote(
            src, wbuf.at[chip, core], sib_send.at[chip], sib_recv.at[chip], me_t, sibling
        )

    def part_copy(chip, d):
        t = frame_at(d)
        return remote(
            part.at[chip, t], inbox.at[chip, d - 1],
            part_send.at[chip, d - 1], part_recv.at[chip, d - 1], t, me_r,
        )

    def rows_copy(turn, d):
        return remote(
            st_rows.at[turn, me_r], st_rows.at[turn, me_r],
            sr_send.at[turn, d - 1], sr_recv.at[turn, d - 1], me_t, row_at(d),
        )

    def tm_copy(turn, d):
        return remote(
            st_tm.at[turn, me_t], st_tm.at[turn, me_t],
            st_send.at[turn, d - 1], st_recv.at[turn, d - 1], frame_at(d), me_r,
        )

    def rows_start(turn, first, second):
        blank = jnp.zeros((6, channels), jnp.float32)
        st_rows[turn, me_r] = jnp.concatenate([first, second, blank], axis=0)
        for d in range(1, count):
            rows_copy(turn, d).start()

    def tm_start(turn):
        for d in range(1, count):
            rows_copy(turn, d).wait_recv()
        total = st_rows[turn, 0]
        for r in range(1, count):
            total = total + st_rows[turn, r]
        st_tm[turn, me_t] = total
        for d in range(1, frames):
            tm_copy(turn, d).start()

    def tm_finish(turn):
        for d in range(1, frames):
            tm_copy(turn, d).wait_recv()
        total = st_tm[turn, 0]
        for t in range(1, frames):
            total = total + st_tm[turn, t]
        return total

    barrier = pltpu.get_barrier_semaphore()
    for d in range(1, count):
        pl.semaphore_signal(barrier, inc=1, device_id=(me_t, row_at(d)), device_id_type=MESH)
    for d in range(1, frames):
        pl.semaphore_signal(barrier, inc=1, device_id=(frame_at(d), me_r), device_id_type=MESH)
    pl.semaphore_wait(barrier, count + frames - 2)

    for side in range(2):
        to_chip = z + (1 if side == 0 else -1)

        @pl.when((to_chip >= 0) & (to_chip < chips))
        def _():
            z_copy(side, 1, z, True).start()

    for d in range(1, frames):
        ct_copy(d).start()
    sib_copy(z, True).start()
    own_ct = pltpu.make_async_copy(
        ct.at[:, :, lanes(me_t)], fine.at[me_t, pl.ds(1, 2)], local_sem.at[0]
    )
    own_w = pltpu.make_async_copy(w, wbuf.at[z, core], local_sem.at[1])
    own_ct.start()
    own_w.start()

    features = lat[...].astype(jnp.float32)
    rows_start(
        0,
        jnp.sum(features, axis=0, keepdims=True),
        jnp.sum(features * features, axis=0, keepdims=True),
    )
    shift = per_group.bit_length() - 1
    left = lax.shift_right_logical(lax.broadcasted_iota(jnp.int32, (channels, channels), 0), shift)
    right = lax.shift_right_logical(lax.broadcasted_iota(jnp.int32, (channels, channels), 1), shift)
    member[...] = jnp.where(left == right, 1.0, 0.0).astype(jnp.bfloat16)
    edge = jnp.zeros((8, width), jnp.float32)
    for u in range(6):
        pad[u, 0:8] = edge
        pad[u, fine_cols + 8 : fine_cols + 16] = edge

    @pl.when(me_r == 0)
    def _():
        fine[:, 0] = jnp.zeros((frames, fine_cols, width), jnp.bfloat16)

    @pl.when(me_r == count - 1)
    def _():
        fine[:, 3] = jnp.zeros((frames, fine_cols, width), jnp.bfloat16)

    own_ct.wait()
    for d in range(1, frames):
        ct_copy(d).wait_recv()

    @pl.when(me_r > 0)
    def _():
        rim_copy(0).start()

    @pl.when(me_r < count - 1)
    def _():
        rim_copy(1).start()

    tm_start(0)
    own_w.wait()

    def arrive(step):
        for side in range(2):
            sign = 1 if side == 0 else -1
            chip = z - sign * step
            to_chip = z + sign

            @pl.when((chip >= 0) & (chip < chips))
            def _():
                z_copy(side, step, chip, False).wait_recv()

                @pl.when((to_chip >= 0) & (to_chip < chips))
                def _():
                    z_copy(side, step + 1, chip, False).start()

                sib_copy(chip, False).start()

    def prepare():
        @pl.when(me_r < count - 1)
        def _():
            rim_copy(0).wait_recv()

        @pl.when(me_r > 0)
        def _():
            rim_copy(1).wait_recv()

        for b in range(3):
            rows = [
                fine[t, 2 - b].astype(jnp.float32) + fine[t, 3 - b].astype(jnp.float32)
                for t in range(frames)
            ]
            early = rows[0] + rows[1]
            for u, value in enumerate(rows + [early, early + rows[2]]):
                pad[u, 8 : fine_cols + 8] = value
            for u in range(6):
                lines = [pad[u, pl.ds(7 + k, low_cols, stride=2), :] for k in range(4)]
                for c in range(3):
                    box = lines[2 - c] + lines[3 - c]
                    high = box.astype(jnp.bfloat16)
                    low = (box - high.astype(jnp.float32)).astype(jnp.bfloat16)
                    tap = slice((3 * b + c) * width, (3 * b + c + 1) * width)
                    stack[u, 0:low_cols, tap] = high
                    stack[u, low_cols : 2 * low_cols, tap] = low

        totals = tm_finish(0)
        scale = 1.0 / (cells * per_group)
        means = group_totals(totals, member[...]) * scale
        mean = means[0:1]
        inv = lax.rsqrt(means[1:2] - mean * mean + 1e-06)
        chan[0:1] = inv
        centred = (lat[...].astype(jnp.float32) - mean) * inv
        normed[...] = centred
        pre = centred * gain[...] + bias[...]
        sg = 1.0 / (1.0 + jnp.exp(-pre))
        slope[...] = sg * (1.0 + pre * (1.0 - sg))

    def process(chip):
        sib_copy(chip, False).wait_recv()
        for a in range(3):
            for k in range(9):
                for side in range(2):
                    wcat[a, side * half : (side + 1) * half, k * width : (k + 1) * width] = wbuf[
                        chip, side, 9 * a + k
                    ]
        for t in range(frames):
            total = None
            for a, u in (((2, 0), (1, 4), (0, 5)) if t == 0 else zip((2, 1, 0), range(t, frames))):
                product = lax.dot_general(
                    stack[u], wcat[a], (((1,), (1,)), ((), ())), preferred_element_type=jnp.float32
                )
                total = product if total is None else total + product
            part[chip, t] = total[:low_cols] + total[low_cols:]
        for d in range(1, frames):
            part_copy(chip, d).start()

    def turn(k, carry):
        @pl.when(k + 1 < chips)
        def _():
            arrive(k + 1)

        @pl.when(k == 0)
        def _():
            prepare()

        def one_side(side, inner):
            chip = z + (2 * side - 1) * k

            @pl.when((chip >= 0) & (chip < chips) & ((k > 0) | (side == 0)))
            def _():
                process(chip)

            return inner

        return lax.fori_loop(0, 2, one_side, carry)

    lax.fori_loop(0, chips, turn, 0)

    sums, scaled_sums = [], []
    for chip in range(chips):
        span = slice(2 * half * chip, 2 * half * (chip + 1))
        up = part[chip, me_t]
        for d in range(1, frames):
            part_copy(chip, d).wait_recv()
            up = up + inbox[chip, d - 1]
        act = up * slope[:, span]
        out[:, span] = act
        sums.append(jnp.sum(act, axis=0, keepdims=True))
        scaled_sums.append(jnp.sum(act * normed[:, span], axis=0, keepdims=True))
    rows_start(1, jnp.concatenate(sums, axis=1), jnp.concatenate(scaled_sums, axis=1))
    tm_start(1)
    totals = tm_finish(1)
    bias_out[...] = totals[0:1] * (1.0 / cells)
    gain_out[...] = totals[1:2] * (1.0 / cells)
    means = group_totals(totals * gain[...], member[...]) * (1.0 / (cells * per_group))
    inv = chan[0:1]
    out[...] = inv * (out[...] * gain[...] - means[0:1] - normed[...] * means[1:2])

    for d in range(1, frames):
        ct_copy(d).wait_send()
        for chip in range(chips):
            part_copy(chip, d).wait_send()
        for turn_index in range(2):
            tm_copy(turn_index, d).wait_send()
    for d in range(1, count):
        for turn_index in range(2):
            rows_copy(turn_index, d).wait_send()

    @pl.when(me_r > 0)
    def _():
        rim_copy(0).wait_send()

    @pl.when(me_r < count - 1)
    def _():
        rim_copy(1).wait_send()

    for chip in range(chips):
        sib_copy(chip, False).wait_send()
    for side in range(2):
        sign = 1 if side == 0 else -1
        to_chip = z + sign
        for step in range(1, chips):
            chip = z - sign * (step - 1)

            @pl.when((to_chip >= 0) & (to_chip < chips) & (chip >= 0) & (chip < chips))
            def _():
                z_copy(side, step, chip, False).wait_send()


def fused(latent, norm_gain, norm_bias, conv_weight, cotangent):
    frames = lax.axis_size("tm")
    count = lax.axis_size("rows")
    low_cols, channels = latent.shape[2:]
    fine_cols = cotangent.shape[2]
    half, width = conv_weight.shape[3:]
    chips = count // 2
    f32, bf16 = jnp.float32, jnp.bfloat16
    dma = pltpu.SemaphoreType.DMA
    body = functools.partial(
        fused_kernel, frames, count, channels // GROUPS, frames * count * low_cols
    )
    vmem = pl.BlockSpec(memory_space=pltpu.VMEM)
    products = chips * 9 * 2 * low_cols * 9 * width * 2 * half
    grad, gain_grad, bias_grad = pl.pallas_call(
        body,
        out_shape=(
            jax.ShapeDtypeStruct((low_cols, channels), f32),
            jax.ShapeDtypeStruct((1, channels), f32),
            jax.ShapeDtypeStruct((1, channels), f32),
        ),
        in_specs=[vmem] * 5,
        out_specs=(vmem,) * 3,
        scratch_shapes=[
            pltpu.VMEM((frames, 4, fine_cols, width), bf16),
            pltpu.VMEM((chips, 2, 27, half, width), bf16),
            pltpu.VMEM((3, 2 * half, 9 * width), bf16),
            pltpu.VMEM((6, 2 * low_cols, 9 * width), bf16),
            pltpu.VMEM((6, fine_cols + 16, width), f32),
            pltpu.VMEM((chips, frames, low_cols, 2 * half), f32),
            pltpu.VMEM((chips, frames - 1, low_cols, 2 * half), f32),
            pltpu.VMEM((low_cols, channels), f32),
            pltpu.VMEM((low_cols, channels), f32),
            pltpu.VMEM((8, channels), f32),
            pltpu.VMEM((channels, channels), bf16),
            pltpu.VMEM((2, count, 8, channels), f32),
            pltpu.VMEM((2, frames, 8, channels), f32),
            dma((2,)),
            dma((frames - 1,)),
            dma((frames - 1,)),
            dma((2,)),
            dma((2,)),
            dma((2, chips)),
            dma((2, chips)),
            dma((chips,)),
            dma((chips,)),
            dma((chips, frames - 1)),
            dma((chips, frames - 1)),
            dma((2, count - 1)),
            dma((2, count - 1)),
            dma((2, frames - 1)),
            dma((2, frames - 1)),
        ],
        compiler_params=pltpu.CompilerParams(
            collective_id=0, has_side_effects=True, vmem_limit_bytes=48 * 1024 * 1024
        ),
        cost_estimate=pl.CostEstimate(
            flops=2 * products, bytes_accessed=2 * 1024 * 1024, transcendentals=low_cols * channels
        ),
    )(
        cotangent.reshape(cotangent.shape[1:]),
        conv_weight.reshape((27, half, width)),
        latent.reshape((low_cols, channels)),
        norm_gain.reshape((1, channels)),
        norm_bias.reshape((1, channels)),
    )
    return grad.reshape(latent.shape), gain_grad.reshape(-1), bias_grad.reshape(-1)


def on_device(latent, norm_gain, norm_bias, conv_weight, cotangent):
    half, width = conv_weight.shape[3:]
    per_group = latent.shape[3] // GROUPS
    fits = (
        lax.axis_size("tm") == 4
        and latent.shape[1] == 1
        and lax.axis_size("rows") % 2 == 0
        and half % 64 == 0
        and width % 128 == 0
        and latent.shape[2] % 16 == 0
        and per_group & (per_group - 1) == 0
    )
    run = fused if fits else spread_out
    return run(latent, norm_gain, norm_bias, conv_weight, cotangent)


def solution(mesh):
    placed = (
        P("tm", "rows", None, None),
        P(),
        P(),
        P(None, None, None, "rows", "tm"),
        P("tm", "rows", None, None),
    )
    return jax.shard_map(
        on_device,
        mesh=mesh,
        in_specs=placed,
        out_specs=(P("tm", "rows", None, None), P(), P()),
        check_vma=False,
    )
```

```python
import functools

import jax
import jax.numpy as jnp
from jax import lax
from jax.experimental import pallas as pl
from jax.experimental.pallas import tpu as pltpu
from jax.sharding import PartitionSpec as P

GROUPS = 32


def split_pair(value):
    high = lax.reduce_precision(value, 8, 7)
    return high.astype(jnp.bfloat16), (value - high).astype(jnp.bfloat16)


def row_rims(block):
    count = lax.axis_size("rows")
    forward = [(i, i + 1) for i in range(count - 1)]
    backward = [(target, source) for source, target in forward]
    low = lax.ppermute(block[:, -1:], "rows", forward)
    high = lax.ppermute(block[:, :1], "rows", backward)
    return jnp.concatenate([low, block, high], axis=1)


def box_sums(block):
    wide = jnp.pad(block.astype(jnp.float32), ((0, 0), (0, 0), (1, 1), (0, 0)))
    rows = wide[:, :-1] + wide[:, 1:]
    return rows[:, :, :-1] + rows[:, :, 1:]


def up_grad_part(boxes, weights, low_rows, low_cols):
    frames = boxes.shape[0]
    early = [boxes[:1]]
    for t in (1, 2):
        early.append(early[-1] + boxes[t : t + 1])
    total = None
    for a in range(3):
        stack = jnp.concatenate([early[2 - a], boxes[3 - a :]], axis=0)
        taps = []
        for b in range(3):
            for c in range(3):
                taps.append(
                    stack[:, 2 - b : 1 - b + 2 * low_rows : 2, 2 - c : 1 - c + 2 * low_cols : 2]
                )
        wide = jnp.concatenate(taps, axis=-1)
        kernel = jnp.concatenate([weights[a, b, c] for b in range(3) for c in range(3)], axis=-1)
        high, low = split_pair(wide)
        product = sum(
            lax.dot_general(
                part, kernel, (((3,), (1,)), ((), ())), preferred_element_type=jnp.float32
            )
            for part in (high, low)
        )
        product = jnp.pad(product, ((0, frames - product.shape[0]), (0, 0), (0, 0), (0, 0)))
        total = product if total is None else total + product
    return total


def spread_out(latent, norm_gain, norm_bias, conv_weight, cotangent):
    frames_all = lax.axis_size("tm")
    rows_all = lax.axis_size("rows")
    low_rows, low_cols, channels = latent.shape[1:]
    per_group = channels // GROUPS
    cell_count = frames_all * rows_all * low_rows * low_cols
    weights = lax.all_gather(conv_weight, "rows", axis=3, tiled=True)
    swapped = lax.all_to_all(cotangent, "tm", split_axis=3, concat_axis=0, tiled=True)
    part = up_grad_part(box_sums(row_rims(swapped)), weights, low_rows, low_cols)
    up_grad = lax.psum_scatter(part, "tm", scatter_dimension=0, tiled=True)
    features = latent.astype(jnp.float32)
    sum_x = jnp.sum(features, axis=(0, 1, 2))
    sum_sq = jnp.sum(features * features, axis=(0, 1, 2))
    total_x, total_sq = lax.psum((sum_x, sum_sq), ("tm", "rows"))
    group_x = total_x.reshape(GROUPS, per_group).sum(axis=1)
    group_sq = total_sq.reshape(GROUPS, per_group).sum(axis=1)
    group_mean = group_x / (cell_count * per_group)
    group_var = group_sq / (cell_count * per_group) - group_mean * group_mean
    inv_std = lax.rsqrt(group_var + 1e-06)
    mean_chan = jnp.repeat(group_mean, per_group)
    inv_chan = jnp.repeat(inv_std, per_group)
    normed = (features - mean_chan) * inv_chan
    pre = normed * norm_gain + norm_bias
    sigmoid_pre = jax.nn.sigmoid(pre)
    act_grad = up_grad * sigmoid_pre * (1.0 + pre * (1.0 - sigmoid_pre))
    sum_act, sum_scaled = lax.psum(
        (jnp.sum(act_grad, axis=(0, 1, 2)), jnp.sum(act_grad * normed, axis=(0, 1, 2))),
        ("tm", "rows"),
    )
    gain_grad = sum_scaled / cell_count
    bias_grad = sum_act / cell_count
    mean_q = (norm_gain * sum_act).reshape(GROUPS, per_group).sum(axis=1) / (cell_count * per_group)
    mean_qn = (norm_gain * sum_scaled).reshape(GROUPS, per_group).sum(axis=1) / (
        cell_count * per_group
    )
    latent_grad = inv_chan * (
        act_grad * norm_gain
        - jnp.repeat(mean_q, per_group)
        - normed * jnp.repeat(mean_qn, per_group)
    )
    return (latent_grad, gain_grad, bias_grad)


MESH = pl.DeviceIdType.MESH


def group_totals(value, member):
    first = value.astype(jnp.bfloat16).astype(jnp.float32)
    rest = value - first
    second = rest.astype(jnp.bfloat16).astype(jnp.float32)
    third = rest - second
    parts = jnp.concatenate([first, second, third, jnp.zeros_like(first)], axis=0)
    sums = jnp.dot(parts.astype(jnp.bfloat16), member, preferred_element_type=jnp.float32)
    rows = value.shape[0]
    return sums[:rows] + sums[rows : 2 * rows] + sums[2 * rows : 3 * rows]


def fused_kernel(
    frames, count, per_group, cells,
    ct, w, lat_hbm, gain_hbm, bias_hbm,
    out, gain_out, bias_out,
    lat, gain, bias, acc, fine, wbuf, wcat, stack, pad, part, inbox, normed, slope, chan, member, st_rows, st_tm,
    local_sem, ct_send, ct_recv, rim_send, rim_recv, z_send, z_recv, sib_send, sib_recv,
    part_send, part_recv, sr_send, sr_recv, st_send, st_recv,
):
    chips = count // 2
    low_cols, channels = lat.shape
    fine_cols = ct.shape[1]
    width = w.shape[2]
    half = w.shape[1]
    me_t = lax.axis_index("tm")
    me_r = lax.axis_index("rows")
    z = lax.div(me_r, 2)
    core = lax.rem(me_r, 2)
    sibling = me_r + 1 - 2 * core

    def remote(src, dst, send, recv, t, r):
        return pltpu.make_async_remote_copy(
            src_ref=src, dst_ref=dst, send_sem=send, recv_sem=recv,
            device_id=(t, r), device_id_type=MESH,
        )

    def frame_at(d):
        return lax.rem(me_t + d, frames)

    def row_at(d):
        return lax.rem(me_r + d, count)

    def lanes(t):
        return pl.ds(pl.multiple_of(t * width, width), width)

    def ct_copy(d):
        t = frame_at(d)
        return remote(
            ct.at[:, :, lanes(t)], fine.at[me_t, pl.ds(1, 2)],
            ct_send.at[d - 1], ct_recv.at[d - 1], t, me_r,
        )

    def rim_copy(side):
        return remote(
            fine.at[:, 1 + side], fine.at[:, 3 - 3 * side],
            rim_send.at[side], rim_recv.at[side], me_t, row_at(count - 1 + 2 * side),
        )

    def piece(chip, a):
        return wbuf.at[chip, core, pl.ds(9 * a, 9)]

    def z_copy(side, step, chip, a, first):
        return remote(
            w.at[pl.ds(9 * a, 9)] if first else piece(chip, a), piece(chip, a),
            z_send.at[side, step - 1, a], z_recv.at[side, step - 1, a],
            me_t, row_at(2 + side * (count - 4)),
        )

    def sib_copy(chip, a, first):
        return remote(
            w.at[pl.ds(9 * a, 9)] if first else piece(chip, a), piece(chip, a),
            sib_send.at[chip, a], sib_recv.at[chip, a], me_t, sibling,
        )

    def part_copy(chip, d):
        t = frame_at(d)
        return remote(
            part.at[chip, t], inbox.at[chip, d - 1],
            part_send.at[chip, d - 1], part_recv.at[chip, d - 1], t, me_r,
        )

    def rows_copy(turn, d):
        return remote(
            st_rows.at[turn, me_r], st_rows.at[turn, me_r],
            sr_send.at[turn, d - 1], sr_recv.at[turn, d - 1], me_t, row_at(d),
        )

    def tm_copy(turn, d):
        return remote(
            st_tm.at[turn, me_t], st_tm.at[turn, me_t],
            st_send.at[turn, d - 1], st_recv.at[turn, d - 1], frame_at(d), me_r,
        )

    def rows_start(turn, first, second):
        st_rows[turn, me_r] = jnp.concatenate(
            [line[:, k : k + 128] for line in (first, second) for k in range(0, channels, 128)],
            axis=0,
        )
        for d in range(1, count):
            rows_copy(turn, d).start()

    def tm_start(turn):
        for d in range(1, count):
            rows_copy(turn, d).wait_recv()
        total = st_rows[turn, 0]
        for r in range(1, count):
            total = total + st_rows[turn, r]
        st_tm[turn, me_t] = total
        for d in range(1, frames):
            tm_copy(turn, d).start()

    def tm_finish(turn):
        for d in range(1, frames):
            tm_copy(turn, d).wait_recv()
        total = st_tm[turn, 0]
        for t in range(1, frames):
            total = total + st_tm[turn, t]
        lines = channels // 128
        first, second = (
            jnp.concatenate([total[k : k + 1] for k in range(start, start + lines)], axis=1)
            for start in (0, lines)
        )
        return jnp.concatenate([first, second, jnp.zeros((6, channels), jnp.float32)], axis=0)

    own = [
        pltpu.make_async_copy(src, dst, local_sem.at[k])
        for k, (src, dst) in enumerate(
            [
                (lat_hbm, lat),
                (gain_hbm, gain),
                (bias_hbm, bias),
                (ct.at[:, :, lanes(me_t)], fine.at[me_t, pl.ds(1, 2)]),
                (w, wbuf.at[z, core]),
            ]
        )
    ]
    for copy in own:
        copy.start()
    barrier = pltpu.get_barrier_semaphore()
    for d in range(1, count):
        pl.semaphore_signal(barrier, inc=1, device_id=(me_t, row_at(d)), device_id_type=MESH)
    for d in range(1, frames):
        pl.semaphore_signal(barrier, inc=1, device_id=(frame_at(d), me_r), device_id_type=MESH)
    pl.semaphore_wait(barrier, count + frames - 2)

    for side in range(2):
        to_chip = z + (1 if side == 0 else -1)

        @pl.when((to_chip >= 0) & (to_chip < chips))
        def _():
            for a in (2, 1, 0):
                z_copy(side, 1, z, a, True).start()

    for d in range(1, frames):
        ct_copy(d).start()
    for a in (2, 1, 0):
        sib_copy(z, a, True).start()

    for copy in own[:3]:
        copy.wait()
    features = lat[...].astype(jnp.float32)
    rows_start(
        0,
        jnp.sum(features, axis=0, keepdims=True),
        jnp.sum(features * features, axis=0, keepdims=True),
    )
    shift = per_group.bit_length() - 1
    left = lax.shift_right_logical(lax.broadcasted_iota(jnp.int32, (channels, channels), 0), shift)
    right = lax.shift_right_logical(lax.broadcasted_iota(jnp.int32, (channels, channels), 1), shift)
    member[...] = jnp.where(left == right, 1.0, 0.0).astype(jnp.bfloat16)
    edge = jnp.zeros((8, width), jnp.float32)
    for u in range(6):
        pad[u, 0:8] = edge
        pad[u, fine_cols + 8 : fine_cols + 16] = edge

    @pl.when(me_r == 0)
    def _():
        fine[:, 0] = jnp.zeros((frames, fine_cols, width), jnp.bfloat16)

    @pl.when(me_r == count - 1)
    def _():
        fine[:, 3] = jnp.zeros((frames, fine_cols, width), jnp.bfloat16)

    own[3].wait()
    for d in range(1, frames):
        ct_copy(d).wait_recv()

    @pl.when(me_r > 0)
    def _():
        rim_copy(0).start()

    @pl.when(me_r < count - 1)
    def _():
        rim_copy(1).start()

    tm_start(0)
    own[4].wait()

    def arrive(step):
        for a in (2, 1, 0):
            for side in range(2):
                sign = 1 if side == 0 else -1
                chip = z - sign * step
                to_chip = z + sign

                @pl.when((chip >= 0) & (chip < chips))
                def _():
                    z_copy(side, step, chip, a, False).wait_recv()

                    @pl.when((to_chip >= 0) & (to_chip < chips))
                    def _():
                        z_copy(side, step + 1, chip, a, False).start()

                    sib_copy(chip, a, False).start()

    def prepare():
        @pl.when(me_r < count - 1)
        def _():
            rim_copy(0).wait_recv()

        @pl.when(me_r > 0)
        def _():
            rim_copy(1).wait_recv()

        for b in range(3):
            rows = [
                fine[t, 2 - b].astype(jnp.float32) + fine[t, 3 - b].astype(jnp.float32)
                for t in range(frames)
            ]
            early = rows[0] + rows[1]
            for u, value in enumerate(rows + [early, early + rows[2]]):
                pad[u, 8 : fine_cols + 8] = value
            for u in range(6):
                lines = [pad[u, pl.ds(7 + k, low_cols, stride=2), :] for k in range(4)]
                for c in range(3):
                    box = lines[2 - c] + lines[3 - c]
                    high = box.astype(jnp.bfloat16)
                    low = (box - high.astype(jnp.float32)).astype(jnp.bfloat16)
                    tap = slice((3 * b + c) * width, (3 * b + c + 1) * width)
                    stack[u, 0:low_cols, tap] = high
                    stack[u, low_cols : 2 * low_cols, tap] = low

        totals = tm_finish(0)
        scale = 1.0 / (cells * per_group)
        means = group_totals(totals, member[...]) * scale
        mean = means[0:1]
        inv = lax.rsqrt(means[1:2] - mean * mean + 1e-06)
        chan[0:1] = inv
        centred = (lat[...].astype(jnp.float32) - mean) * inv
        normed[...] = centred
        pre = centred * gain[...] + bias[...]
        sg = 1.0 / (1.0 + jnp.exp(-pre))
        slope[...] = sg * (1.0 + pre * (1.0 - sg))

    def process(chip, side, k):
        for a in (2, 1, 0):

            @pl.when(k == chips - 1)
            def _():
                z_copy(side, chips - 1, chip, a, False).wait_recv()
                sib_copy(chip, a, False).start()

            sib_copy(chip, a, False).wait_recv()
            for tap in range(9):
                for part_of in range(2):
                    wcat[
                        a, part_of * half : (part_of + 1) * half, tap * width : (tap + 1) * width
                    ] = wbuf[chip, part_of, 9 * a + tap]
            for t in range(min(frames, a + 2) - 1, -1, -1):
                unit = (5, 4, 0)[a] if t == 0 else t + 2 - a
                total = lax.dot_general(
                    stack[unit], wcat[a], (((1,), (1,)), ((), ())),
                    preferred_element_type=jnp.float32,
                )
                if a < 2:
                    total = total + acc[t]
                if a > max(0, t - 1):
                    acc[t] = total
                    continue
                part[chip, t] = total[:low_cols] + total[low_cols:]

                @pl.when(me_t != t)
                def _():
                    part_copy(chip, lax.rem(t - me_t + frames, frames)).start()

    def turn(k, carry):
        @pl.when(k + 1 < chips - 1)
        def _():
            arrive(k + 1)

        @pl.when(k == 0)
        def _():
            prepare()

        def one_side(side, inner):
            chip = z + (2 * side - 1) * k

            @pl.when((chip >= 0) & (chip < chips) & ((k > 0) | (side == 0)))
            def _():
                process(chip, side, k)

            return inner

        return lax.fori_loop(0, 2, one_side, carry)

    lax.fori_loop(0, chips, turn, 0)

    sums, scaled_sums = [], []
    for chip in range(chips):
        span = slice(2 * half * chip, 2 * half * (chip + 1))
        up = part[chip, me_t]
        for d in range(1, frames):
            part_copy(chip, d).wait_recv()
            up = up + inbox[chip, d - 1]
        act = up * slope[:, span]
        out[:, span] = act
        sums.append(jnp.sum(act, axis=0, keepdims=True))
        scaled_sums.append(jnp.sum(act * normed[:, span], axis=0, keepdims=True))
    rows_start(1, jnp.concatenate(sums, axis=1), jnp.concatenate(scaled_sums, axis=1))
    tm_start(1)
    totals = tm_finish(1)
    bias_out[...] = totals[0:1] * (1.0 / cells)
    gain_out[...] = totals[1:2] * (1.0 / cells)
    means = group_totals(totals * gain[...], member[...]) * (1.0 / (cells * per_group))
    inv = chan[0:1]
    out[...] = inv * (out[...] * gain[...] - means[0:1] - normed[...] * means[1:2])

    for d in range(1, frames):
        ct_copy(d).wait_send()
        for chip in range(chips):
            part_copy(chip, d).wait_send()
        for turn_index in range(2):
            tm_copy(turn_index, d).wait_send()
    for d in range(1, count):
        for turn_index in range(2):
            rows_copy(turn_index, d).wait_send()

    @pl.when(me_r > 0)
    def _():
        rim_copy(0).wait_send()

    @pl.when(me_r < count - 1)
    def _():
        rim_copy(1).wait_send()

    for chip in range(chips):
        for a in range(3):
            sib_copy(chip, a, False).wait_send()
    for side in range(2):
        sign = 1 if side == 0 else -1
        to_chip = z + sign
        for step in range(1, chips):
            chip = z - sign * (step - 1)

            @pl.when((to_chip >= 0) & (to_chip < chips) & (chip >= 0) & (chip < chips))
            def _():
                for a in range(3):
                    z_copy(side, step, chip, a, False).wait_send()


def fused(latent, norm_gain, norm_bias, conv_weight, cotangent):
    frames = lax.axis_size("tm")
    count = lax.axis_size("rows")
    low_cols, channels = latent.shape[2:]
    fine_cols = cotangent.shape[2]
    half, width = conv_weight.shape[3:]
    chips = count // 2
    f32, bf16 = jnp.float32, jnp.bfloat16
    dma = pltpu.SemaphoreType.DMA
    body = functools.partial(
        fused_kernel, frames, count, channels // GROUPS, frames * count * low_cols
    )
    vmem = pl.BlockSpec(memory_space=pltpu.VMEM)
    products = chips * 9 * 2 * low_cols * 9 * width * 2 * half
    grad, gain_grad, bias_grad = pl.pallas_call(
        body,
        out_shape=(
            jax.ShapeDtypeStruct((low_cols, channels), f32),
            jax.ShapeDtypeStruct((1, channels), f32),
            jax.ShapeDtypeStruct((1, channels), f32),
        ),
        in_specs=[pl.BlockSpec(memory_space=pltpu.HBM)] * 5,
        out_specs=(vmem,) * 3,
        scratch_shapes=[
            pltpu.VMEM((low_cols, channels), bf16),
            pltpu.VMEM((1, channels), f32),
            pltpu.VMEM((1, channels), f32),
            pltpu.VMEM((frames - 1, 2 * low_cols, 2 * half), f32),
            pltpu.VMEM((frames, 4, fine_cols, width), bf16),
            pltpu.VMEM((chips, 2, 27, half, width), bf16),
            pltpu.VMEM((3, 2 * half, 9 * width), bf16),
            pltpu.VMEM((6, 2 * low_cols, 9 * width), bf16),
            pltpu.VMEM((6, fine_cols + 16, width), f32),
            pltpu.VMEM((chips, frames, low_cols, 2 * half), f32),
            pltpu.VMEM((chips, frames - 1, low_cols, 2 * half), f32),
            pltpu.VMEM((low_cols, channels), f32),
            pltpu.VMEM((low_cols, channels), f32),
            pltpu.VMEM((8, channels), f32),
            pltpu.VMEM((channels, channels), bf16),
            pltpu.VMEM((2, count, channels // 64, 128), f32),
            pltpu.VMEM((2, frames, channels // 64, 128), f32),
            dma((5,)),
            dma((frames - 1,)),
            dma((frames - 1,)),
            dma((2,)),
            dma((2,)),
            dma((2, chips - 1, 3)),
            dma((2, chips - 1, 3)),
            dma((chips, 3)),
            dma((chips, 3)),
            dma((chips, frames - 1)),
            dma((chips, frames - 1)),
            dma((2, count - 1)),
            dma((2, count - 1)),
            dma((2, frames - 1)),
            dma((2, frames - 1)),
        ],
        compiler_params=pltpu.CompilerParams(
            collective_id=0, has_side_effects=True, vmem_limit_bytes=62 * 1024 * 1024
        ),
        cost_estimate=pl.CostEstimate(
            flops=2 * products, bytes_accessed=2 * 1024 * 1024, transcendentals=low_cols * channels
        ),
    )(
        cotangent.reshape(cotangent.shape[1:]),
        conv_weight.reshape((27, half, width)),
        latent.reshape((low_cols, channels)),
        norm_gain.reshape((1, channels)),
        norm_bias.reshape((1, channels)),
    )
    return grad.reshape(latent.shape), gain_grad.reshape(-1), bias_grad.reshape(-1)


def on_device(latent, norm_gain, norm_bias, conv_weight, cotangent):
    half, width = conv_weight.shape[3:]
    per_group = latent.shape[3] // GROUPS
    fits = (
        lax.axis_size("tm") == 4
        and latent.shape[1] == 1
        and latent.shape[3] % 512 == 0
        and lax.axis_size("rows") % 2 == 0
        and half % 64 == 0
        and width % 128 == 0
        and latent.shape[2] % 16 == 0
        and per_group & (per_group - 1) == 0
    )
    run = fused if fits else spread_out
    return run(latent, norm_gain, norm_bias, conv_weight, cotangent)


def solution(mesh):
    placed = (
        P("tm", "rows", None, None),
        P(),
        P(),
        P(None, None, None, "rows", "tm"),
        P("tm", "rows", None, None),
    )
    return jax.shard_map(
        on_device,
        mesh=mesh,
        in_specs=placed,
        out_specs=(P("tm", "rows", None, None), P(), P()),
        check_vma=False,
    )
```

```python
import functools

import jax
import jax.numpy as jnp
from jax import lax
from jax.experimental import pallas as pl
from jax.experimental.pallas import tpu as pltpu
from jax.sharding import PartitionSpec as P

GROUPS = 32


def split_pair(value):
    high = lax.reduce_precision(value, 8, 7)
    return high.astype(jnp.bfloat16), (value - high).astype(jnp.bfloat16)


def row_rims(block):
    count = lax.axis_size("rows")
    forward = [(i, i + 1) for i in range(count - 1)]
    backward = [(target, source) for source, target in forward]
    low = lax.ppermute(block[:, -1:], "rows", forward)
    high = lax.ppermute(block[:, :1], "rows", backward)
    return jnp.concatenate([low, block, high], axis=1)


def box_sums(block):
    wide = jnp.pad(block.astype(jnp.float32), ((0, 0), (0, 0), (1, 1), (0, 0)))
    rows = wide[:, :-1] + wide[:, 1:]
    return rows[:, :, :-1] + rows[:, :, 1:]


def up_grad_part(boxes, weights, low_rows, low_cols):
    frames = boxes.shape[0]
    early = [boxes[:1]]
    for t in (1, 2):
        early.append(early[-1] + boxes[t : t + 1])
    total = None
    for a in range(3):
        stack = jnp.concatenate([early[2 - a], boxes[3 - a :]], axis=0)
        taps = []
        for b in range(3):
            for c in range(3):
                taps.append(
                    stack[:, 2 - b : 1 - b + 2 * low_rows : 2, 2 - c : 1 - c + 2 * low_cols : 2]
                )
        wide = jnp.concatenate(taps, axis=-1)
        kernel = jnp.concatenate([weights[a, b, c] for b in range(3) for c in range(3)], axis=-1)
        high, low = split_pair(wide)
        product = sum(
            lax.dot_general(
                part, kernel, (((3,), (1,)), ((), ())), preferred_element_type=jnp.float32
            )
            for part in (high, low)
        )
        product = jnp.pad(product, ((0, frames - product.shape[0]), (0, 0), (0, 0), (0, 0)))
        total = product if total is None else total + product
    return total


def spread_out(latent, norm_gain, norm_bias, conv_weight, cotangent):
    frames_all = lax.axis_size("tm")
    rows_all = lax.axis_size("rows")
    low_rows, low_cols, channels = latent.shape[1:]
    per_group = channels // GROUPS
    cell_count = frames_all * rows_all * low_rows * low_cols
    weights = lax.all_gather(conv_weight, "rows", axis=3, tiled=True)
    swapped = lax.all_to_all(cotangent, "tm", split_axis=3, concat_axis=0, tiled=True)
    part = up_grad_part(box_sums(row_rims(swapped)), weights, low_rows, low_cols)
    up_grad = lax.psum_scatter(part, "tm", scatter_dimension=0, tiled=True)
    features = latent.astype(jnp.float32)
    sum_x = jnp.sum(features, axis=(0, 1, 2))
    sum_sq = jnp.sum(features * features, axis=(0, 1, 2))
    total_x, total_sq = lax.psum((sum_x, sum_sq), ("tm", "rows"))
    group_x = total_x.reshape(GROUPS, per_group).sum(axis=1)
    group_sq = total_sq.reshape(GROUPS, per_group).sum(axis=1)
    group_mean = group_x / (cell_count * per_group)
    group_var = group_sq / (cell_count * per_group) - group_mean * group_mean
    inv_std = lax.rsqrt(group_var + 1e-06)
    mean_chan = jnp.repeat(group_mean, per_group)
    inv_chan = jnp.repeat(inv_std, per_group)
    normed = (features - mean_chan) * inv_chan
    pre = normed * norm_gain + norm_bias
    sigmoid_pre = jax.nn.sigmoid(pre)
    act_grad = up_grad * sigmoid_pre * (1.0 + pre * (1.0 - sigmoid_pre))
    sum_act, sum_scaled = lax.psum(
        (jnp.sum(act_grad, axis=(0, 1, 2)), jnp.sum(act_grad * normed, axis=(0, 1, 2))),
        ("tm", "rows"),
    )
    gain_grad = sum_scaled / cell_count
    bias_grad = sum_act / cell_count
    mean_q = (norm_gain * sum_act).reshape(GROUPS, per_group).sum(axis=1) / (cell_count * per_group)
    mean_qn = (norm_gain * sum_scaled).reshape(GROUPS, per_group).sum(axis=1) / (
        cell_count * per_group
    )
    latent_grad = inv_chan * (
        act_grad * norm_gain
        - jnp.repeat(mean_q, per_group)
        - normed * jnp.repeat(mean_qn, per_group)
    )
    return (latent_grad, gain_grad, bias_grad)


MESH = pl.DeviceIdType.MESH


def group_totals(value, member):
    first = value.astype(jnp.bfloat16).astype(jnp.float32)
    rest = value - first
    second = rest.astype(jnp.bfloat16).astype(jnp.float32)
    third = rest - second
    parts = jnp.concatenate([first, second, third, jnp.zeros_like(first)], axis=0)
    sums = jnp.dot(parts.astype(jnp.bfloat16), member, preferred_element_type=jnp.float32)
    rows = value.shape[0]
    return sums[:rows] + sums[rows : 2 * rows] + sums[2 * rows : 3 * rows]


def fused_kernel(
    frames, count, per_group, cells,
    ct, w, lat_hbm, gain_hbm, bias_hbm,
    out, gain_out, bias_out,
    lat, gain, bias, acc, fine, wbuf, wcat, stack, pad, part, inbox, normed, slope, chan, member, st_rows, st_tm,
    local_sem, ct_send, ct_recv, rim_send, rim_recv, z_send, z_recv, sib_send, sib_recv,
    part_send, part_recv, sr_send, sr_recv, st_send, st_recv,
):
    chips = count // 2
    low_cols, channels = lat.shape
    fine_cols = ct.shape[1]
    width = w.shape[2]
    half = w.shape[1]
    me_t = lax.axis_index("tm")
    me_r = lax.axis_index("rows")
    z = lax.div(me_r, 2)
    core = lax.rem(me_r, 2)
    sibling = me_r + 1 - 2 * core

    def remote(src, dst, send, recv, t, r):
        return pltpu.make_async_remote_copy(
            src_ref=src, dst_ref=dst, send_sem=send, recv_sem=recv,
            device_id=(t, r), device_id_type=MESH,
        )

    def frame_at(d):
        return lax.rem(me_t + d, frames)

    def row_at(d):
        return lax.rem(me_r + d, count)

    def lanes(t):
        return pl.ds(pl.multiple_of(t * width, width), width)

    def ct_copy(d):
        t = frame_at(d)
        return remote(
            ct.at[:, :, lanes(t)], fine.at[me_t, pl.ds(1, 2)],
            ct_send.at[d - 1], ct_recv.at[d - 1], t, me_r,
        )

    def rim_copy(side):
        return remote(
            fine.at[:, 1 + side], fine.at[:, 3 - 3 * side],
            rim_send.at[side], rim_recv.at[side], me_t, row_at(count - 1 + 2 * side),
        )

    def piece(chip, a):
        return wbuf.at[chip, core, pl.ds(9 * a, 9)]

    def z_copy(side, step, chip, a, first):
        return remote(
            w.at[pl.ds(9 * a, 9)] if first else piece(chip, a), piece(chip, a),
            z_send.at[side, step - 1, a], z_recv.at[side, step - 1, a],
            me_t, row_at(2 + side * (count - 4)),
        )

    def sib_copy(chip, a, first):
        return remote(
            w.at[pl.ds(9 * a, 9)] if first else piece(chip, a), piece(chip, a),
            sib_send.at[chip, a], sib_recv.at[chip, a], me_t, sibling,
        )

    def part_copy(chip, d):
        t = frame_at(d)
        return remote(
            part.at[chip, t], inbox.at[chip, d - 1],
            part_send.at[chip, d - 1], part_recv.at[chip, d - 1], t, me_r,
        )

    def rows_copy(turn, d):
        return remote(
            st_rows.at[turn, me_r], st_rows.at[turn, me_r],
            sr_send.at[turn, d - 1], sr_recv.at[turn, d - 1], me_t, row_at(d),
        )

    def tm_copy(turn, d):
        return remote(
            st_tm.at[turn, me_t], st_tm.at[turn, me_t],
            st_send.at[turn, d - 1], st_recv.at[turn, d - 1], frame_at(d), me_r,
        )

    def rows_start(turn, first, second):
        st_rows[turn, me_r] = jnp.concatenate(
            [line[:, k : k + 128] for line in (first, second) for k in range(0, channels, 128)],
            axis=0,
        )
        for d in range(1, count):
            rows_copy(turn, d).start()

    def tm_start(turn):
        for d in range(1, count):
            rows_copy(turn, d).wait_recv()
        total = st_rows[turn, 0]
        for r in range(1, count):
            total = total + st_rows[turn, r]
        st_tm[turn, me_t] = total
        for d in range(1, frames):
            tm_copy(turn, d).start()

    def tm_finish(turn):
        for d in range(1, frames):
            tm_copy(turn, d).wait_recv()
        total = st_tm[turn, 0]
        for t in range(1, frames):
            total = total + st_tm[turn, t]
        lines = channels // 128
        first, second = (
            jnp.concatenate([total[k : k + 1] for k in range(start, start + lines)], axis=1)
            for start in (0, lines)
        )
        return jnp.concatenate([first, second, jnp.zeros((6, channels), jnp.float32)], axis=0)

    own = [
        pltpu.make_async_copy(src, dst, local_sem.at[k])
        for k, (src, dst) in enumerate(
            [
                (lat_hbm, lat),
                (gain_hbm, gain),
                (bias_hbm, bias),
                (ct.at[:, :, lanes(me_t)], fine.at[me_t, pl.ds(1, 2)]),
                (w, wbuf.at[z, core]),
            ]
        )
    ]
    for copy in own:
        copy.start()
    barrier = pltpu.get_barrier_semaphore()
    for d in range(1, count):
        pl.semaphore_signal(barrier, inc=1, device_id=(me_t, row_at(d)), device_id_type=MESH)
    for d in range(1, frames):
        pl.semaphore_signal(barrier, inc=1, device_id=(frame_at(d), me_r), device_id_type=MESH)
    pl.semaphore_wait(barrier, count + frames - 2)

    for side in range(2):
        to_chip = z + (1 if side == 0 else -1)

        @pl.when((to_chip >= 0) & (to_chip < chips))
        def _():
            for a in (2, 1, 0):
                z_copy(side, 1, z, a, True).start()

    for d in range(1, frames):
        ct_copy(d).start()
    for a in (2, 1, 0):
        sib_copy(z, a, True).start()

    for copy in own[:3]:
        copy.wait()
    features = lat[...].astype(jnp.float32)
    rows_start(
        0,
        jnp.sum(features, axis=0, keepdims=True),
        jnp.sum(features * features, axis=0, keepdims=True),
    )
    shift = per_group.bit_length() - 1
    left = lax.shift_right_logical(lax.broadcasted_iota(jnp.int32, (channels, channels), 0), shift)
    right = lax.shift_right_logical(lax.broadcasted_iota(jnp.int32, (channels, channels), 1), shift)
    member[...] = jnp.where(left == right, 1.0, 0.0).astype(jnp.bfloat16)
    edge = jnp.zeros((8, width), jnp.float32)
    for u in range(6):
        pad[u, 0:8] = edge
        pad[u, fine_cols + 8 : fine_cols + 16] = edge

    @pl.when(me_r == 0)
    def _():
        fine[:, 0] = jnp.zeros((frames, fine_cols, width), jnp.bfloat16)

    @pl.when(me_r == count - 1)
    def _():
        fine[:, 3] = jnp.zeros((frames, fine_cols, width), jnp.bfloat16)

    own[3].wait()
    for d in range(1, frames):
        ct_copy(d).wait_recv()

    @pl.when(me_r > 0)
    def _():
        rim_copy(0).start()

    @pl.when(me_r < count - 1)
    def _():
        rim_copy(1).start()

    tm_start(0)
    own[4].wait()

    def arrive(step):
        for a in (2, 1, 0):
            for side in range(2):
                sign = 1 if side == 0 else -1
                chip = z - sign * step
                to_chip = z + sign

                @pl.when((chip >= 0) & (chip < chips))
                def _():
                    z_copy(side, step, chip, a, False).wait_recv()

                    @pl.when((to_chip >= 0) & (to_chip < chips))
                    def _():
                        z_copy(side, step + 1, chip, a, False).start()

                    sib_copy(chip, a, False).start()

    def prepare():
        @pl.when(me_r < count - 1)
        def _():
            rim_copy(0).wait_recv()

        @pl.when(me_r > 0)
        def _():
            rim_copy(1).wait_recv()

        for b in range(3):
            rows = [
                fine[t, 2 - b].astype(jnp.float32) + fine[t, 3 - b].astype(jnp.float32)
                for t in range(frames)
            ]
            early = rows[0] + rows[1]
            for u, value in enumerate(rows + [early, early + rows[2]]):
                pad[u, 8 : fine_cols + 8] = value
            for u in range(6):
                lines = [pad[u, pl.ds(7 + k, low_cols, stride=2), :] for k in range(4)]
                for c in range(3):
                    box = lines[2 - c] + lines[3 - c]
                    high = box.astype(jnp.bfloat16)
                    low = (box - high.astype(jnp.float32)).astype(jnp.bfloat16)
                    tap = slice((3 * b + c) * width, (3 * b + c + 1) * width)
                    for slot in ((0,), (1,), (2, 5), (3, 6, 8), (4,), (7,))[u]:
                        stack[slot, 0:low_cols, tap] = high
                        stack[slot, low_cols : 2 * low_cols, tap] = low

        totals = tm_finish(0)
        scale = 1.0 / (cells * per_group)
        means = group_totals(totals, member[...]) * scale
        mean = means[0:1]
        inv = lax.rsqrt(means[1:2] - mean * mean + 1e-06)
        chan[0:1] = inv
        centred = (lat[...].astype(jnp.float32) - mean) * inv
        normed[...] = centred
        pre = centred * gain[...] + bias[...]
        sg = 1.0 / (1.0 + jnp.exp(-pre))
        slope[...] = sg * (1.0 + pre * (1.0 - sg))

    def process(chip, side, k):
        for a in (2, 1, 0):

            @pl.when(k == chips - 1)
            def _():
                z_copy(side, chips - 1, chip, a, False).wait_recv()
                sib_copy(chip, a, False).start()

            sib_copy(chip, a, False).wait_recv()
            for tap in range(9):
                for part_of in range(2):
                    wcat[
                        a, part_of * half : (part_of + 1) * half, tap * width : (tap + 1) * width
                    ] = wbuf[chip, part_of, 9 * a + tap]
            first_slot = (7, 4, 0)[a]
            product = lax.dot_general(
                stack[first_slot : first_slot + a + 2].reshape((a + 2) * 2 * low_cols, 9 * width),
                wcat[a],
                (((1,), (1,)), ((), ())),
                preferred_element_type=jnp.float32,
            )
            for t in range(a + 1, -1, -1):
                total = product[2 * low_cols * t : 2 * low_cols * (t + 1)]
                if a < 2:
                    total = total + acc[t]
                if a > max(0, t - 1):
                    acc[t] = total
                    continue
                part[chip, t] = total[:low_cols] + total[low_cols:]

                @pl.when(me_t != t)
                def _():
                    part_copy(chip, lax.rem(t - me_t + frames, frames)).start()

    def turn(k, carry):
        @pl.when(k + 1 < chips - 1)
        def _():
            arrive(k + 1)

        @pl.when(k == 0)
        def _():
            prepare()

        def one_side(side, inner):
            chip = z + (2 * side - 1) * k

            @pl.when((chip >= 0) & (chip < chips) & ((k > 0) | (side == 0)))
            def _():
                process(chip, side, k)

            return inner

        return lax.fori_loop(0, 2, one_side, carry)

    lax.fori_loop(0, chips, turn, 0)

    sums, scaled_sums = [], []
    for chip in range(chips):
        span = slice(2 * half * chip, 2 * half * (chip + 1))
        up = part[chip, me_t]
        for d in range(1, frames):
            part_copy(chip, d).wait_recv()
            up = up + inbox[chip, d - 1]
        act = up * slope[:, span]
        out[:, span] = act
        sums.append(jnp.sum(act, axis=0, keepdims=True))
        scaled_sums.append(jnp.sum(act * normed[:, span], axis=0, keepdims=True))
    rows_start(1, jnp.concatenate(sums, axis=1), jnp.concatenate(scaled_sums, axis=1))
    tm_start(1)
    totals = tm_finish(1)
    bias_out[...] = totals[0:1] * (1.0 / cells)
    gain_out[...] = totals[1:2] * (1.0 / cells)
    means = group_totals(totals * gain[...], member[...]) * (1.0 / (cells * per_group))
    inv = chan[0:1]
    out[...] = inv * (out[...] * gain[...] - means[0:1] - normed[...] * means[1:2])

    for d in range(1, frames):
        ct_copy(d).wait_send()
        for chip in range(chips):
            part_copy(chip, d).wait_send()
        for turn_index in range(2):
            tm_copy(turn_index, d).wait_send()
    for d in range(1, count):
        for turn_index in range(2):
            rows_copy(turn_index, d).wait_send()

    @pl.when(me_r > 0)
    def _():
        rim_copy(0).wait_send()

    @pl.when(me_r < count - 1)
    def _():
        rim_copy(1).wait_send()

    for chip in range(chips):
        for a in range(3):
            sib_copy(chip, a, False).wait_send()
    for side in range(2):
        sign = 1 if side == 0 else -1
        to_chip = z + sign
        for step in range(1, chips):
            chip = z - sign * (step - 1)

            @pl.when((to_chip >= 0) & (to_chip < chips) & (chip >= 0) & (chip < chips))
            def _():
                for a in range(3):
                    z_copy(side, step, chip, a, False).wait_send()


def fused(latent, norm_gain, norm_bias, conv_weight, cotangent):
    frames = lax.axis_size("tm")
    count = lax.axis_size("rows")
    low_cols, channels = latent.shape[2:]
    fine_cols = cotangent.shape[2]
    half, width = conv_weight.shape[3:]
    chips = count // 2
    f32, bf16 = jnp.float32, jnp.bfloat16
    dma = pltpu.SemaphoreType.DMA
    body = functools.partial(
        fused_kernel, frames, count, channels // GROUPS, frames * count * low_cols
    )
    vmem = pl.BlockSpec(memory_space=pltpu.VMEM)
    products = chips * 9 * 2 * low_cols * 9 * width * 2 * half
    grad, gain_grad, bias_grad = pl.pallas_call(
        body,
        out_shape=(
            pltpu.VMEM((low_cols, channels), f32),
            pltpu.VMEM((1, channels), f32),
            pltpu.VMEM((1, channels), f32),
        ),
        in_specs=[pl.BlockSpec(memory_space=pltpu.HBM)] * 5,
        out_specs=(vmem,) * 3,
        scratch_shapes=[
            pltpu.VMEM((low_cols, channels), bf16),
            pltpu.VMEM((1, channels), f32),
            pltpu.VMEM((1, channels), f32),
            pltpu.VMEM((frames - 1, 2 * low_cols, 2 * half), f32),
            pltpu.VMEM((frames, 4, fine_cols, width), bf16),
            pltpu.VMEM((chips, 2, 27, half, width), bf16),
            pltpu.VMEM((3, 2 * half, 9 * width), bf16),
            pltpu.VMEM((9, 2 * low_cols, 9 * width), bf16),
            pltpu.VMEM((6, fine_cols + 16, width), f32),
            pltpu.VMEM((chips, frames, low_cols, 2 * half), f32),
            pltpu.VMEM((chips, frames - 1, low_cols, 2 * half), f32),
            pltpu.VMEM((low_cols, channels), f32),
            pltpu.VMEM((low_cols, channels), f32),
            pltpu.VMEM((8, channels), f32),
            pltpu.VMEM((channels, channels), bf16),
            pltpu.VMEM((2, count, channels // 64, 128), f32),
            pltpu.VMEM((2, frames, channels // 64, 128), f32),
            dma((5,)),
            dma((frames - 1,)),
            dma((frames - 1,)),
            dma((2,)),
            dma((2,)),
            dma((2, chips - 1, 3)),
            dma((2, chips - 1, 3)),
            dma((chips, 3)),
            dma((chips, 3)),
            dma((chips, frames - 1)),
            dma((chips, frames - 1)),
            dma((2, count - 1)),
            dma((2, count - 1)),
            dma((2, frames - 1)),
            dma((2, frames - 1)),
        ],
        compiler_params=pltpu.CompilerParams(
            collective_id=0, has_side_effects=True, vmem_limit_bytes=60 * 1024 * 1024
        ),
        cost_estimate=pl.CostEstimate(
            flops=2 * products, bytes_accessed=2 * 1024 * 1024, transcendentals=low_cols * channels
        ),
    )(
        cotangent.reshape(cotangent.shape[1:]),
        conv_weight.reshape((27, half, width)),
        latent.reshape((low_cols, channels)),
        norm_gain.reshape((1, channels)),
        norm_bias.reshape((1, channels)),
    )
    return grad.reshape(latent.shape), gain_grad.reshape(-1), bias_grad.reshape(-1)


def on_device(latent, norm_gain, norm_bias, conv_weight, cotangent):
    half, width = conv_weight.shape[3:]
    per_group = latent.shape[3] // GROUPS
    fits = (
        lax.axis_size("tm") == 4
        and latent.shape[1] == 1
        and latent.shape[3] % 512 == 0
        and lax.axis_size("rows") % 2 == 0
        and half % 64 == 0
        and width % 128 == 0
        and latent.shape[2] % 16 == 0
        and per_group & (per_group - 1) == 0
    )
    run = fused if fits else spread_out
    return run(latent, norm_gain, norm_bias, conv_weight, cotangent)


def solution(mesh):
    placed = (
        P("tm", "rows", None, None),
        P(),
        P(),
        P(None, None, None, "rows", "tm"),
        P("tm", "rows", None, None),
    )
    return jax.shard_map(
        on_device,
        mesh=mesh,
        in_specs=placed,
        out_specs=(P("tm", "rows", None, None), P(), P()),
        check_vma=False,
    )
```

```python
import functools

import jax
import jax.numpy as jnp
from jax import lax
from jax.experimental import pallas as pl
from jax.experimental.pallas import tpu as pltpu
from jax.sharding import PartitionSpec as P

GROUPS = 32


def split_pair(value):
    high = lax.reduce_precision(value, 8, 7)
    return high.astype(jnp.bfloat16), (value - high).astype(jnp.bfloat16)


def row_rims(block):
    count = lax.axis_size("rows")
    forward = [(i, i + 1) for i in range(count - 1)]
    backward = [(target, source) for source, target in forward]
    low = lax.ppermute(block[:, -1:], "rows", forward)
    high = lax.ppermute(block[:, :1], "rows", backward)
    return jnp.concatenate([low, block, high], axis=1)


def box_sums(block):
    wide = jnp.pad(block.astype(jnp.float32), ((0, 0), (0, 0), (1, 1), (0, 0)))
    rows = wide[:, :-1] + wide[:, 1:]
    return rows[:, :, :-1] + rows[:, :, 1:]


def up_grad_part(boxes, weights, low_rows, low_cols):
    frames = boxes.shape[0]
    early = [boxes[:1]]
    for t in (1, 2):
        early.append(early[-1] + boxes[t : t + 1])
    total = None
    for a in range(3):
        stack = jnp.concatenate([early[2 - a], boxes[3 - a :]], axis=0)
        taps = []
        for b in range(3):
            for c in range(3):
                taps.append(
                    stack[:, 2 - b : 1 - b + 2 * low_rows : 2, 2 - c : 1 - c + 2 * low_cols : 2]
                )
        wide = jnp.concatenate(taps, axis=-1)
        kernel = jnp.concatenate([weights[a, b, c] for b in range(3) for c in range(3)], axis=-1)
        high, low = split_pair(wide)
        product = sum(
            lax.dot_general(
                part, kernel, (((3,), (1,)), ((), ())), preferred_element_type=jnp.float32
            )
            for part in (high, low)
        )
        product = jnp.pad(product, ((0, frames - product.shape[0]), (0, 0), (0, 0), (0, 0)))
        total = product if total is None else total + product
    return total


def spread_out(latent, norm_gain, norm_bias, conv_weight, cotangent):
    frames_all = lax.axis_size("tm")
    rows_all = lax.axis_size("rows")
    low_rows, low_cols, channels = latent.shape[1:]
    per_group = channels // GROUPS
    cell_count = frames_all * rows_all * low_rows * low_cols
    weights = lax.all_gather(conv_weight, "rows", axis=3, tiled=True)
    swapped = lax.all_to_all(cotangent, "tm", split_axis=3, concat_axis=0, tiled=True)
    part = up_grad_part(box_sums(row_rims(swapped)), weights, low_rows, low_cols)
    up_grad = lax.psum_scatter(part, "tm", scatter_dimension=0, tiled=True)
    features = latent.astype(jnp.float32)
    sum_x = jnp.sum(features, axis=(0, 1, 2))
    sum_sq = jnp.sum(features * features, axis=(0, 1, 2))
    total_x, total_sq = lax.psum((sum_x, sum_sq), ("tm", "rows"))
    group_x = total_x.reshape(GROUPS, per_group).sum(axis=1)
    group_sq = total_sq.reshape(GROUPS, per_group).sum(axis=1)
    group_mean = group_x / (cell_count * per_group)
    group_var = group_sq / (cell_count * per_group) - group_mean * group_mean
    inv_std = lax.rsqrt(group_var + 1e-06)
    mean_chan = jnp.repeat(group_mean, per_group)
    inv_chan = jnp.repeat(inv_std, per_group)
    normed = (features - mean_chan) * inv_chan
    pre = normed * norm_gain + norm_bias
    sigmoid_pre = jax.nn.sigmoid(pre)
    act_grad = up_grad * sigmoid_pre * (1.0 + pre * (1.0 - sigmoid_pre))
    sum_act, sum_scaled = lax.psum(
        (jnp.sum(act_grad, axis=(0, 1, 2)), jnp.sum(act_grad * normed, axis=(0, 1, 2))),
        ("tm", "rows"),
    )
    gain_grad = sum_scaled / cell_count
    bias_grad = sum_act / cell_count
    mean_q = (norm_gain * sum_act).reshape(GROUPS, per_group).sum(axis=1) / (cell_count * per_group)
    mean_qn = (norm_gain * sum_scaled).reshape(GROUPS, per_group).sum(axis=1) / (
        cell_count * per_group
    )
    latent_grad = inv_chan * (
        act_grad * norm_gain
        - jnp.repeat(mean_q, per_group)
        - normed * jnp.repeat(mean_qn, per_group)
    )
    return (latent_grad, gain_grad, bias_grad)


MESH = pl.DeviceIdType.MESH


def group_totals(value, member):
    first = value.astype(jnp.bfloat16).astype(jnp.float32)
    rest = value - first
    second = rest.astype(jnp.bfloat16).astype(jnp.float32)
    third = rest - second
    parts = jnp.concatenate([first, second, third, jnp.zeros_like(first)], axis=0)
    sums = jnp.dot(parts.astype(jnp.bfloat16), member, preferred_element_type=jnp.float32)
    rows = value.shape[0]
    return sums[:rows] + sums[rows : 2 * rows] + sums[2 * rows : 3 * rows]


def fused_kernel(
    frames, count, per_group, cells,
    ct, w, lat_hbm, gain_hbm, bias_hbm,
    out, sums_out,
    lat, gain, bias, acc, fine, wbuf, wcat, stack, pad, part, inbox, normed, slope, chan, member, st_rows, st_tm,
    local_sem, ct_send, ct_recv, rim_send, rim_recv, z_send, z_recv, sib_send, sib_recv,
    part_send, part_recv, sr_send, sr_recv, st_send, st_recv,
):
    chips = count // 2
    low_cols, channels = lat.shape
    fine_cols = ct.shape[1]
    width = w.shape[2]
    half = w.shape[1]
    me_t = lax.axis_index("tm")
    me_r = lax.axis_index("rows")
    z = lax.div(me_r, 2)
    core = lax.rem(me_r, 2)
    sibling = me_r + 1 - 2 * core

    def remote(src, dst, send, recv, t, r):
        return pltpu.make_async_remote_copy(
            src_ref=src, dst_ref=dst, send_sem=send, recv_sem=recv,
            device_id=(t, r), device_id_type=MESH,
        )

    def frame_at(d):
        return lax.rem(me_t + d, frames)

    def row_at(d):
        return lax.rem(me_r + d, count)

    def lanes(t):
        return pl.ds(pl.multiple_of(t * width, width), width)

    def ct_copy(d):
        t = frame_at(d)
        return remote(
            ct.at[:, :, lanes(t)], fine.at[me_t, pl.ds(1, 2)],
            ct_send.at[d - 1], ct_recv.at[d - 1], t, me_r,
        )

    def rim_copy(side):
        return remote(
            fine.at[:, 1 + side], fine.at[:, 3 - 3 * side],
            rim_send.at[side], rim_recv.at[side], me_t, row_at(count - 1 + 2 * side),
        )

    def piece(chip, a):
        return wbuf.at[chip, core, pl.ds(9 * a, 9)]

    def z_copy(side, step, chip, a, first):
        return remote(
            w.at[pl.ds(9 * a, 9)] if first else piece(chip, a), piece(chip, a),
            z_send.at[side, step - 1, a], z_recv.at[side, step - 1, a],
            me_t, row_at(2 + side * (count - 4)),
        )

    def sib_copy(chip, a, first):
        return remote(
            w.at[pl.ds(9 * a, 9)] if first else piece(chip, a), piece(chip, a),
            sib_send.at[chip, a], sib_recv.at[chip, a], me_t, sibling,
        )

    def part_copy(chip, d):
        t = frame_at(d)
        return remote(
            part.at[chip, t], inbox.at[chip, d - 1],
            part_send.at[chip, d - 1], part_recv.at[chip, d - 1], t, me_r,
        )

    def rows_copy(turn, d):
        return remote(
            st_rows.at[turn, me_r], st_rows.at[turn, me_r],
            sr_send.at[turn, d - 1], sr_recv.at[turn, d - 1], me_t, row_at(d),
        )

    def tm_copy(turn, d):
        return remote(
            st_tm.at[turn, me_t], st_tm.at[turn, me_t],
            st_send.at[turn, d - 1], st_recv.at[turn, d - 1], frame_at(d), me_r,
        )

    def rows_start(turn, first, second):
        st_rows[turn, me_r] = jnp.concatenate(
            [line[:, k : k + 128] for line in (first, second) for k in range(0, channels, 128)],
            axis=0,
        )
        for d in range(1, count):
            rows_copy(turn, d).start()

    def tm_start(turn):
        for d in range(1, count):
            rows_copy(turn, d).wait_recv()
        total = st_rows[turn, 0]
        for r in range(1, count):
            total = total + st_rows[turn, r]
        st_tm[turn, me_t] = total
        for d in range(1, frames):
            tm_copy(turn, d).start()

    def tm_finish(turn):
        for d in range(1, frames):
            tm_copy(turn, d).wait_recv()
        total = st_tm[turn, 0]
        for t in range(1, frames):
            total = total + st_tm[turn, t]
        lines = channels // 128
        first, second = (
            jnp.concatenate([total[k : k + 1] for k in range(start, start + lines)], axis=1)
            for start in (0, lines)
        )
        return jnp.concatenate([first, second, jnp.zeros((6, channels), jnp.float32)], axis=0)

    own = [
        pltpu.make_async_copy(src, dst, local_sem.at[k])
        for k, (src, dst) in enumerate(
            [
                (lat_hbm, lat),
                (gain_hbm, gain),
                (bias_hbm, bias),
                (ct.at[:, :, lanes(me_t)], fine.at[me_t, pl.ds(1, 2)]),
                (w, wbuf.at[z, core]),
            ]
        )
    ]
    for copy in own:
        copy.start()
    barrier = pltpu.get_barrier_semaphore()
    for d in range(1, count):
        pl.semaphore_signal(barrier, inc=1, device_id=(me_t, row_at(d)), device_id_type=MESH)
    for d in range(1, frames):
        pl.semaphore_signal(barrier, inc=1, device_id=(frame_at(d), me_r), device_id_type=MESH)
    pl.semaphore_wait(barrier, count + frames - 2)

    for side in range(2):
        to_chip = z + (1 if side == 0 else -1)

        @pl.when((to_chip >= 0) & (to_chip < chips))
        def _():
            for a in (2, 1, 0):
                z_copy(side, 1, z, a, True).start()

    for d in range(1, frames):
        ct_copy(d).start()
    for a in (2, 1, 0):
        sib_copy(z, a, True).start()

    for copy in own[:3]:
        copy.wait()
    features = lat[...].astype(jnp.float32)
    rows_start(
        0,
        jnp.sum(features, axis=0, keepdims=True),
        jnp.sum(features * features, axis=0, keepdims=True),
    )
    shift = per_group.bit_length() - 1
    left = lax.shift_right_logical(lax.broadcasted_iota(jnp.int32, (channels, channels), 0), shift)
    right = lax.shift_right_logical(lax.broadcasted_iota(jnp.int32, (channels, channels), 1), shift)
    member[...] = jnp.where(left == right, 1.0, 0.0).astype(jnp.bfloat16)
    edge = jnp.zeros((8, width), jnp.float32)
    for u in range(6):
        pad[u, 0:8] = edge
        pad[u, fine_cols + 8 : fine_cols + 16] = edge

    @pl.when(me_r == 0)
    def _():
        fine[:, 0] = jnp.zeros((frames, fine_cols, width), jnp.bfloat16)

    @pl.when(me_r == count - 1)
    def _():
        fine[:, 3] = jnp.zeros((frames, fine_cols, width), jnp.bfloat16)

    own[3].wait()
    for d in range(1, frames):
        ct_copy(d).wait_recv()

    @pl.when(me_r > 0)
    def _():
        rim_copy(0).start()

    @pl.when(me_r < count - 1)
    def _():
        rim_copy(1).start()

    tm_start(0)
    own[4].wait()

    def arrive(step):
        for a in (2, 1, 0):
            for side in range(2):
                sign = 1 if side == 0 else -1
                chip = z - sign * step
                to_chip = z + sign

                @pl.when((chip >= 0) & (chip < chips))
                def _():
                    z_copy(side, step, chip, a, False).wait_recv()

                    @pl.when((to_chip >= 0) & (to_chip < chips))
                    def _():
                        z_copy(side, step + 1, chip, a, False).start()

                    sib_copy(chip, a, False).start()

    def prepare():
        @pl.when(me_r < count - 1)
        def _():
            rim_copy(0).wait_recv()

        @pl.when(me_r > 0)
        def _():
            rim_copy(1).wait_recv()

        for b in range(3):
            rows = [
                fine[t, 2 - b].astype(jnp.float32) + fine[t, 3 - b].astype(jnp.float32)
                for t in range(frames)
            ]
            early = rows[0] + rows[1]
            for u, value in enumerate(rows + [early, early + rows[2]]):
                pad[u, 8 : fine_cols + 8] = value
            for u in range(6):
                lines = [pad[u, pl.ds(7 + k, low_cols, stride=2), :] for k in range(4)]
                for c in range(3):
                    box = lines[2 - c] + lines[3 - c]
                    high = box.astype(jnp.bfloat16)
                    low = (box - high.astype(jnp.float32)).astype(jnp.bfloat16)
                    tap = slice((3 * b + c) * width, (3 * b + c + 1) * width)
                    for slot in ((0,), (1,), (2, 5), (3, 6, 8), (4,), (7,))[u]:
                        stack[slot, 0:low_cols, tap] = high
                        stack[slot, low_cols : 2 * low_cols, tap] = low

        totals = tm_finish(0)
        scale = 1.0 / (cells * per_group)
        means = group_totals(totals, member[...]) * scale
        mean = means[0:1]
        inv = lax.rsqrt(means[1:2] - mean * mean + 1e-06)
        chan[0:1] = inv
        centred = (lat[...].astype(jnp.float32) - mean) * inv
        normed[...] = centred
        pre = centred * gain[...] + bias[...]
        sg = 1.0 / (1.0 + jnp.exp(-pre))
        slope[...] = sg * (1.0 + pre * (1.0 - sg))

    def process(chip, side, k):
        for a in (2, 1, 0):

            @pl.when(k == chips - 1)
            def _():
                z_copy(side, chips - 1, chip, a, False).wait_recv()
                sib_copy(chip, a, False).start()

            sib_copy(chip, a, False).wait_recv()
            for tap in range(9):
                for part_of in range(2):
                    wcat[
                        a, part_of * half : (part_of + 1) * half, tap * width : (tap + 1) * width
                    ] = wbuf[chip, part_of, 9 * a + tap]
            first_slot = (7, 4, 0)[a]
            for t in range(a + 1, -1, -1):
                total = lax.dot_general(
                    stack[first_slot + t], wcat[a], (((1,), (1,)), ((), ())),
                    preferred_element_type=jnp.float32,
                )
                if a < 2:
                    total = total + acc[t]
                if a > max(0, t - 1):
                    acc[t] = total
                    continue
                part[chip, t] = total[:low_cols] + total[low_cols:]

                @pl.when(me_t != t)
                def _():
                    part_copy(chip, lax.rem(t - me_t + frames, frames)).start()

    def turn(k, carry):
        @pl.when(k + 1 < chips - 1)
        def _():
            arrive(k + 1)

        @pl.when(k == 0)
        def _():
            prepare()

        def one_side(side, inner):
            chip = z + (2 * side - 1) * k

            @pl.when((chip >= 0) & (chip < chips) & ((k > 0) | (side == 0)))
            def _():
                process(chip, side, k)

            return inner

        return lax.fori_loop(0, 2, one_side, carry)

    lax.fori_loop(0, chips, turn, 0)

    sums, scaled_sums = [], []
    for chip in range(chips):
        span = slice(2 * half * chip, 2 * half * (chip + 1))
        up = part[chip, me_t]
        for d in range(1, frames):
            part_copy(chip, d).wait_recv()
            up = up + inbox[chip, d - 1]
        act = up * slope[:, span]
        out[:, span] = act
        sums.append(jnp.sum(act, axis=0, keepdims=True))
        scaled_sums.append(jnp.sum(act * normed[:, span], axis=0, keepdims=True))
    rows_start(1, jnp.concatenate(sums, axis=1), jnp.concatenate(scaled_sums, axis=1))
    tm_start(1)
    totals = tm_finish(1)
    sums_out[...] = totals * (1.0 / cells)
    means = group_totals(totals * gain[...], member[...]) * (1.0 / (cells * per_group))
    inv = chan[0:1]
    out[...] = inv * (out[...] * gain[...] - means[0:1] - normed[...] * means[1:2])

    for d in range(1, frames):
        ct_copy(d).wait_send()
        for chip in range(chips):
            part_copy(chip, d).wait_send()
        for turn_index in range(2):
            tm_copy(turn_index, d).wait_send()
    for d in range(1, count):
        for turn_index in range(2):
            rows_copy(turn_index, d).wait_send()

    @pl.when(me_r > 0)
    def _():
        rim_copy(0).wait_send()

    @pl.when(me_r < count - 1)
    def _():
        rim_copy(1).wait_send()

    for chip in range(chips):
        for a in range(3):
            sib_copy(chip, a, False).wait_send()
    for side in range(2):
        sign = 1 if side == 0 else -1
        to_chip = z + sign
        for step in range(1, chips):
            chip = z - sign * (step - 1)

            @pl.when((to_chip >= 0) & (to_chip < chips) & (chip >= 0) & (chip < chips))
            def _():
                for a in range(3):
                    z_copy(side, step, chip, a, False).wait_send()


def fused(latent, norm_gain, norm_bias, conv_weight, cotangent):
    frames = lax.axis_size("tm")
    count = lax.axis_size("rows")
    low_cols, channels = latent.shape[2:]
    fine_cols = cotangent.shape[2]
    half, width = conv_weight.shape[3:]
    chips = count // 2
    f32, bf16 = jnp.float32, jnp.bfloat16
    dma = pltpu.SemaphoreType.DMA
    body = functools.partial(
        fused_kernel, frames, count, channels // GROUPS, frames * count * low_cols
    )
    vmem = pl.BlockSpec(memory_space=pltpu.VMEM)
    products = chips * 9 * 2 * low_cols * 9 * width * 2 * half
    grad, sums = pl.pallas_call(
        body,
        out_shape=(
            pltpu.VMEM((low_cols, channels), f32),
            pltpu.VMEM((8, channels), f32),
        ),
        in_specs=[pl.BlockSpec(memory_space=pltpu.HBM)] * 5,
        out_specs=(vmem,) * 2,
        scratch_shapes=[
            pltpu.VMEM((low_cols, channels), bf16),
            pltpu.VMEM((1, channels), f32),
            pltpu.VMEM((1, channels), f32),
            pltpu.VMEM((frames - 1, 2 * low_cols, 2 * half), f32),
            pltpu.VMEM((frames, 4, fine_cols, width), bf16),
            pltpu.VMEM((chips, 2, 27, half, width), bf16),
            pltpu.VMEM((3, 2 * half, 9 * width), bf16),
            pltpu.VMEM((9, 2 * low_cols, 9 * width), bf16),
            pltpu.VMEM((6, fine_cols + 16, width), f32),
            pltpu.VMEM((chips, frames, low_cols, 2 * half), f32),
            pltpu.VMEM((chips, frames - 1, low_cols, 2 * half), f32),
            pltpu.VMEM((low_cols, channels), f32),
            pltpu.VMEM((low_cols, channels), f32),
            pltpu.VMEM((8, channels), f32),
            pltpu.VMEM((channels, channels), bf16),
            pltpu.VMEM((2, count, channels // 64, 128), f32),
            pltpu.VMEM((2, frames, channels // 64, 128), f32),
            dma((5,)),
            dma((frames - 1,)),
            dma((frames - 1,)),
            dma((2,)),
            dma((2,)),
            dma((2, chips - 1, 3)),
            dma((2, chips - 1, 3)),
            dma((chips, 3)),
            dma((chips, 3)),
            dma((chips, frames - 1)),
            dma((chips, frames - 1)),
            dma((2, count - 1)),
            dma((2, count - 1)),
            dma((2, frames - 1)),
            dma((2, frames - 1)),
        ],
        compiler_params=pltpu.CompilerParams(
            collective_id=0, has_side_effects=True, vmem_limit_bytes=60 * 1024 * 1024
        ),
        cost_estimate=pl.CostEstimate(
            flops=2 * products, bytes_accessed=2 * 1024 * 1024, transcendentals=low_cols * channels
        ),
    )(
        cotangent.reshape(cotangent.shape[1:]),
        conv_weight.reshape((27, half, width)),
        latent.reshape((low_cols, channels)),
        norm_gain.reshape((1, channels)),
        norm_bias.reshape((1, channels)),
    )
    return grad.reshape(latent.shape), sums[1], sums[0]


def on_device(latent, norm_gain, norm_bias, conv_weight, cotangent):
    half, width = conv_weight.shape[3:]
    per_group = latent.shape[3] // GROUPS
    fits = (
        lax.axis_size("tm") == 4
        and latent.shape[1] == 1
        and latent.shape[3] % 512 == 0
        and lax.axis_size("rows") % 2 == 0
        and half % 64 == 0
        and width % 128 == 0
        and latent.shape[2] % 16 == 0
        and per_group & (per_group - 1) == 0
    )
    run = fused if fits else spread_out
    return run(latent, norm_gain, norm_bias, conv_weight, cotangent)


def solution(mesh):
    placed = (
        P("tm", "rows", None, None),
        P(),
        P(),
        P(None, None, None, "rows", "tm"),
        P("tm", "rows", None, None),
    )
    return jax.shard_map(
        on_device,
        mesh=mesh,
        in_specs=placed,
        out_specs=(P("tm", "rows", None, None), P(), P()),
        check_vma=False,
    )
```

```python
import functools

import jax
import jax.numpy as jnp
from jax import lax
from jax.experimental import pallas as pl
from jax.experimental.pallas import tpu as pltpu
from jax.sharding import PartitionSpec as P

GROUPS = 32


def split_pair(value):
    high = lax.reduce_precision(value, 8, 7)
    return high.astype(jnp.bfloat16), (value - high).astype(jnp.bfloat16)


def row_rims(block):
    count = lax.axis_size("rows")
    forward = [(i, i + 1) for i in range(count - 1)]
    backward = [(target, source) for source, target in forward]
    low = lax.ppermute(block[:, -1:], "rows", forward)
    high = lax.ppermute(block[:, :1], "rows", backward)
    return jnp.concatenate([low, block, high], axis=1)


def box_sums(block):
    wide = jnp.pad(block.astype(jnp.float32), ((0, 0), (0, 0), (1, 1), (0, 0)))
    rows = wide[:, :-1] + wide[:, 1:]
    return rows[:, :, :-1] + rows[:, :, 1:]


def up_grad_part(boxes, weights, low_rows, low_cols):
    frames = boxes.shape[0]
    early = [boxes[:1]]
    for t in (1, 2):
        early.append(early[-1] + boxes[t : t + 1])
    total = None
    for a in range(3):
        stack = jnp.concatenate([early[2 - a], boxes[3 - a :]], axis=0)
        taps = []
        for b in range(3):
            for c in range(3):
                taps.append(
                    stack[:, 2 - b : 1 - b + 2 * low_rows : 2, 2 - c : 1 - c + 2 * low_cols : 2]
                )
        wide = jnp.concatenate(taps, axis=-1)
        kernel = jnp.concatenate([weights[a, b, c] for b in range(3) for c in range(3)], axis=-1)
        high, low = split_pair(wide)
        product = sum(
            lax.dot_general(
                part, kernel, (((3,), (1,)), ((), ())), preferred_element_type=jnp.float32
            )
            for part in (high, low)
        )
        product = jnp.pad(product, ((0, frames - product.shape[0]), (0, 0), (0, 0), (0, 0)))
        total = product if total is None else total + product
    return total


def spread_out(latent, norm_gain, norm_bias, conv_weight, cotangent):
    frames_all = lax.axis_size("tm")
    rows_all = lax.axis_size("rows")
    low_rows, low_cols, channels = latent.shape[1:]
    per_group = channels // GROUPS
    cell_count = frames_all * rows_all * low_rows * low_cols
    weights = lax.all_gather(conv_weight, "rows", axis=3, tiled=True)
    swapped = lax.all_to_all(cotangent, "tm", split_axis=3, concat_axis=0, tiled=True)
    part = up_grad_part(box_sums(row_rims(swapped)), weights, low_rows, low_cols)
    up_grad = lax.psum_scatter(part, "tm", scatter_dimension=0, tiled=True)
    features = latent.astype(jnp.float32)
    sum_x = jnp.sum(features, axis=(0, 1, 2))
    sum_sq = jnp.sum(features * features, axis=(0, 1, 2))
    total_x, total_sq = lax.psum((sum_x, sum_sq), ("tm", "rows"))
    group_x = total_x.reshape(GROUPS, per_group).sum(axis=1)
    group_sq = total_sq.reshape(GROUPS, per_group).sum(axis=1)
    group_mean = group_x / (cell_count * per_group)
    group_var = group_sq / (cell_count * per_group) - group_mean * group_mean
    inv_std = lax.rsqrt(group_var + 1e-06)
    mean_chan = jnp.repeat(group_mean, per_group)
    inv_chan = jnp.repeat(inv_std, per_group)
    normed = (features - mean_chan) * inv_chan
    pre = normed * norm_gain + norm_bias
    sigmoid_pre = jax.nn.sigmoid(pre)
    act_grad = up_grad * sigmoid_pre * (1.0 + pre * (1.0 - sigmoid_pre))
    sum_act, sum_scaled = lax.psum(
        (jnp.sum(act_grad, axis=(0, 1, 2)), jnp.sum(act_grad * normed, axis=(0, 1, 2))),
        ("tm", "rows"),
    )
    gain_grad = sum_scaled / cell_count
    bias_grad = sum_act / cell_count
    mean_q = (norm_gain * sum_act).reshape(GROUPS, per_group).sum(axis=1) / (cell_count * per_group)
    mean_qn = (norm_gain * sum_scaled).reshape(GROUPS, per_group).sum(axis=1) / (
        cell_count * per_group
    )
    latent_grad = inv_chan * (
        act_grad * norm_gain
        - jnp.repeat(mean_q, per_group)
        - normed * jnp.repeat(mean_qn, per_group)
    )
    return (latent_grad, gain_grad, bias_grad)


MESH = pl.DeviceIdType.MESH


def group_totals(value, member):
    first = value.astype(jnp.bfloat16).astype(jnp.float32)
    rest = value - first
    second = rest.astype(jnp.bfloat16).astype(jnp.float32)
    third = rest - second
    parts = jnp.concatenate([first, second, third, jnp.zeros_like(first)], axis=0)
    sums = jnp.dot(parts.astype(jnp.bfloat16), member, preferred_element_type=jnp.float32)
    rows = value.shape[0]
    return sums[:rows] + sums[rows : 2 * rows] + sums[2 * rows : 3 * rows]


def fused_kernel(
    frames, count, per_group, cells,
    ct, w, lat_hbm, gain_hbm, bias_hbm,
    out, sums_out,
    lat, gain, bias, acc, fine, wbuf, wcat, stack, pad, part, inbox, normed, slope, chan, member, st_all,
    local_sem, ct_send, ct_recv, rim_send, rim_recv, z_send, z_recv, sib_send, sib_recv,
    part_send, part_recv, st_send, st_recv,
):
    chips = count // 2
    low_cols, channels = lat.shape
    fine_cols = ct.shape[1]
    width = w.shape[2]
    half = w.shape[1]
    me_t = lax.axis_index("tm")
    me_r = lax.axis_index("rows")
    z = lax.div(me_r, 2)
    core = lax.rem(me_r, 2)
    sibling = me_r + 1 - 2 * core
    everyone = frames * count
    me = me_t * count + me_r

    def remote(src, dst, send, recv, t, r):
        return pltpu.make_async_remote_copy(
            src_ref=src, dst_ref=dst, send_sem=send, recv_sem=recv,
            device_id=(t, r), device_id_type=MESH,
        )

    def frame_at(d):
        return lax.rem(me_t + d, frames)

    def row_at(d):
        return lax.rem(me_r + d, count)

    def lanes(t):
        return pl.ds(pl.multiple_of(t * width, width), width)

    def ct_copy(d):
        t = frame_at(d)
        return remote(
            ct.at[:, :, lanes(t)], fine.at[me_t, pl.ds(1, 2)],
            ct_send.at[d - 1], ct_recv.at[d - 1], t, me_r,
        )

    def rim_copy(side):
        return remote(
            fine.at[:, 1 + side], fine.at[:, 3 - 3 * side],
            rim_send.at[side], rim_recv.at[side], me_t, row_at(count - 1 + 2 * side),
        )

    def piece(chip, a):
        return wbuf.at[chip, core, pl.ds(9 * a, 9)]

    def z_copy(side, step, chip, a, first):
        return remote(
            w.at[pl.ds(9 * a, 9)] if first else piece(chip, a), piece(chip, a),
            z_send.at[side, step - 1, a], z_recv.at[side, step - 1, a],
            me_t, row_at(2 + side * (count - 4)),
        )

    def sib_copy(chip, a, first):
        return remote(
            w.at[pl.ds(9 * a, 9)] if first else piece(chip, a), piece(chip, a),
            sib_send.at[chip, a], sib_recv.at[chip, a], me_t, sibling,
        )

    def part_copy(chip, d):
        t = frame_at(d)
        return remote(
            part.at[chip, t], inbox.at[chip, d - 1],
            part_send.at[chip, d - 1], part_recv.at[chip, d - 1], t, me_r,
        )

    def peer(d):
        index = lax.rem(me + d, everyone)
        return lax.div(index, count), lax.rem(index, count)

    def sums_copy(turn, d):
        return remote(
            st_all.at[turn, me], st_all.at[turn, me],
            st_send.at[turn, d - 1], st_recv.at[turn, d - 1], *peer(d),
        )

    def each_peer(action):
        def step(d, carry):
            action(d)
            return carry

        lax.fori_loop(1, everyone, step, 0)

    def sums_start(turn, first, second):
        st_all[turn, me] = jnp.concatenate(
            [line[:, k : k + 128] for line in (first, second) for k in range(0, channels, 128)],
            axis=0,
        )
        each_peer(lambda d: sums_copy(turn, d).start())

    def sums_finish(turn):
        each_peer(lambda d: sums_copy(turn, d).wait_recv())
        total = st_all[turn, 0]
        for k in range(1, everyone):
            total = total + st_all[turn, k]
        lines = channels // 128
        first, second = (
            jnp.concatenate([total[k : k + 1] for k in range(start, start + lines)], axis=1)
            for start in (0, lines)
        )
        return jnp.concatenate([first, second, jnp.zeros((6, channels), jnp.float32)], axis=0)

    own = [
        pltpu.make_async_copy(src, dst, local_sem.at[k])
        for k, (src, dst) in enumerate(
            [
                (lat_hbm, lat),
                (gain_hbm, gain),
                (bias_hbm, bias),
                (ct.at[:, :, lanes(me_t)], fine.at[me_t, pl.ds(1, 2)]),
                (w, wbuf.at[z, core]),
            ]
        )
    ]
    for copy in own:
        copy.start()
    barrier = pltpu.get_barrier_semaphore()
    each_peer(
        lambda d: pl.semaphore_signal(barrier, inc=1, device_id=peer(d), device_id_type=MESH)
    )
    pl.semaphore_wait(barrier, everyone - 1)

    for side in range(2):
        to_chip = z + (1 if side == 0 else -1)

        @pl.when((to_chip >= 0) & (to_chip < chips))
        def _():
            for a in (2, 1, 0):
                z_copy(side, 1, z, a, True).start()

    for d in range(1, frames):
        ct_copy(d).start()
    for a in (2, 1, 0):
        sib_copy(z, a, True).start()

    for copy in own[:3]:
        copy.wait()
    features = lat[...].astype(jnp.float32)
    sums_start(
        0,
        jnp.sum(features, axis=0, keepdims=True),
        jnp.sum(features * features, axis=0, keepdims=True),
    )
    shift = per_group.bit_length() - 1
    left = lax.shift_right_logical(lax.broadcasted_iota(jnp.int32, (channels, channels), 0), shift)
    right = lax.shift_right_logical(lax.broadcasted_iota(jnp.int32, (channels, channels), 1), shift)
    member[...] = jnp.where(left == right, 1.0, 0.0).astype(jnp.bfloat16)
    edge = jnp.zeros((8, width), jnp.float32)
    for u in range(6):
        pad[u, 0:8] = edge
        pad[u, fine_cols + 8 : fine_cols + 16] = edge

    @pl.when(me_r == 0)
    def _():
        fine[:, 0] = jnp.zeros((frames, fine_cols, width), jnp.bfloat16)

    @pl.when(me_r == count - 1)
    def _():
        fine[:, 3] = jnp.zeros((frames, fine_cols, width), jnp.bfloat16)

    own[3].wait()
    for d in range(1, frames):
        ct_copy(d).wait_recv()

    @pl.when(me_r > 0)
    def _():
        rim_copy(0).start()

    @pl.when(me_r < count - 1)
    def _():
        rim_copy(1).start()

    own[4].wait()

    def arrive(step):
        for a in (2, 1, 0):
            for side in range(2):
                sign = 1 if side == 0 else -1
                chip = z - sign * step
                to_chip = z + sign

                @pl.when((chip >= 0) & (chip < chips))
                def _():
                    z_copy(side, step, chip, a, False).wait_recv()

                    @pl.when((to_chip >= 0) & (to_chip < chips))
                    def _():
                        z_copy(side, step + 1, chip, a, False).start()

                    sib_copy(chip, a, False).start()

    def prepare():
        @pl.when(me_r < count - 1)
        def _():
            rim_copy(0).wait_recv()

        @pl.when(me_r > 0)
        def _():
            rim_copy(1).wait_recv()

        for b in range(3):
            rows = [
                fine[t, 2 - b].astype(jnp.float32) + fine[t, 3 - b].astype(jnp.float32)
                for t in range(frames)
            ]
            early = rows[0] + rows[1]
            for u, value in enumerate(rows + [early, early + rows[2]]):
                pad[u, 8 : fine_cols + 8] = value
            for u in range(6):
                lines = [pad[u, pl.ds(7 + k, low_cols, stride=2), :] for k in range(4)]
                for c in range(3):
                    box = lines[2 - c] + lines[3 - c]
                    high = box.astype(jnp.bfloat16)
                    low = (box - high.astype(jnp.float32)).astype(jnp.bfloat16)
                    tap = slice((3 * b + c) * width, (3 * b + c + 1) * width)
                    for slot in ((0,), (1,), (2, 5), (3, 6, 8), (4,), (7,))[u]:
                        stack[slot, 0:low_cols, tap] = high
                        stack[slot, low_cols : 2 * low_cols, tap] = low

        totals = sums_finish(0)
        scale = 1.0 / (cells * per_group)
        means = group_totals(totals, member[...]) * scale
        mean = means[0:1]
        inv = lax.rsqrt(means[1:2] - mean * mean + 1e-06)
        chan[0:1] = inv
        centred = (lat[...].astype(jnp.float32) - mean) * inv
        normed[...] = centred
        pre = centred * gain[...] + bias[...]
        sg = 1.0 / (1.0 + jnp.exp(-pre))
        slope[...] = sg * (1.0 + pre * (1.0 - sg))

    def process(chip, side, k):
        for a in (2, 1, 0):

            @pl.when(k == chips - 1)
            def _():
                z_copy(side, chips - 1, chip, a, False).wait_recv()
                sib_copy(chip, a, False).start()

            sib_copy(chip, a, False).wait_recv()
            for tap in range(9):
                for part_of in range(2):
                    wcat[
                        a, part_of * half : (part_of + 1) * half, tap * width : (tap + 1) * width
                    ] = wbuf[chip, part_of, 9 * a + tap]
            first_slot = (7, 4, 0)[a]
            for t in range(a + 1, -1, -1):
                total = lax.dot_general(
                    stack[first_slot + t], wcat[a], (((1,), (1,)), ((), ())),
                    preferred_element_type=jnp.float32,
                )
                if a < 2:
                    total = total + acc[t]
                if a > max(0, t - 1):
                    acc[t] = total
                    continue
                part[chip, t] = total[:low_cols] + total[low_cols:]

                @pl.when(me_t != t)
                def _():
                    part_copy(chip, lax.rem(t - me_t + frames, frames)).start()

    def turn(k, carry):
        @pl.when(k + 1 < chips - 1)
        def _():
            arrive(k + 1)

        @pl.when(k == 0)
        def _():
            prepare()

        def one_side(side, inner):
            chip = z + (2 * side - 1) * k

            @pl.when((chip >= 0) & (chip < chips) & ((k > 0) | (side == 0)))
            def _():
                process(chip, side, k)

            return inner

        return lax.fori_loop(0, 2, one_side, carry)

    lax.fori_loop(0, chips, turn, 0)

    sums, scaled_sums = [], []
    for chip in range(chips):
        span = slice(2 * half * chip, 2 * half * (chip + 1))
        up = part[chip, me_t]
        for d in range(1, frames):
            part_copy(chip, d).wait_recv()
            up = up + inbox[chip, d - 1]
        act = up * slope[:, span]
        out[:, span] = act
        sums.append(jnp.sum(act, axis=0, keepdims=True))
        scaled_sums.append(jnp.sum(act * normed[:, span], axis=0, keepdims=True))
    sums_start(1, jnp.concatenate(sums, axis=1), jnp.concatenate(scaled_sums, axis=1))
    totals = sums_finish(1)
    sums_out[...] = totals * (1.0 / cells)
    means = group_totals(totals * gain[...], member[...]) * (1.0 / (cells * per_group))
    inv = chan[0:1]
    out[...] = inv * (out[...] * gain[...] - means[0:1] - normed[...] * means[1:2])

    for d in range(1, frames):
        ct_copy(d).wait_send()
        for chip in range(chips):
            part_copy(chip, d).wait_send()
    for index in range(2):
        each_peer(lambda d, index=index: sums_copy(index, d).wait_send())

    @pl.when(me_r > 0)
    def _():
        rim_copy(0).wait_send()

    @pl.when(me_r < count - 1)
    def _():
        rim_copy(1).wait_send()

    for chip in range(chips):
        for a in range(3):
            sib_copy(chip, a, False).wait_send()
    for side in range(2):
        sign = 1 if side == 0 else -1
        to_chip = z + sign
        for step in range(1, chips):
            chip = z - sign * (step - 1)

            @pl.when((to_chip >= 0) & (to_chip < chips) & (chip >= 0) & (chip < chips))
            def _():
                for a in range(3):
                    z_copy(side, step, chip, a, False).wait_send()


def fused(latent, norm_gain, norm_bias, conv_weight, cotangent):
    frames = lax.axis_size("tm")
    count = lax.axis_size("rows")
    low_cols, channels = latent.shape[2:]
    fine_cols = cotangent.shape[2]
    half, width = conv_weight.shape[3:]
    chips = count // 2
    f32, bf16 = jnp.float32, jnp.bfloat16
    dma = pltpu.SemaphoreType.DMA
    body = functools.partial(
        fused_kernel, frames, count, channels // GROUPS, frames * count * low_cols
    )
    vmem = pl.BlockSpec(memory_space=pltpu.VMEM)
    products = chips * 9 * 2 * low_cols * 9 * width * 2 * half
    grad, sums = pl.pallas_call(
        body,
        out_shape=(
            pltpu.VMEM((low_cols, channels), f32),
            pltpu.VMEM((8, channels), f32),
        ),
        in_specs=[pl.BlockSpec(memory_space=pltpu.HBM)] * 5,
        out_specs=(vmem,) * 2,
        scratch_shapes=[
            pltpu.VMEM((low_cols, channels), bf16),
            pltpu.VMEM((1, channels), f32),
            pltpu.VMEM((1, channels), f32),
            pltpu.VMEM((frames - 1, 2 * low_cols, 2 * half), f32),
            pltpu.VMEM((frames, 4, fine_cols, width), bf16),
            pltpu.VMEM((chips, 2, 27, half, width), bf16),
            pltpu.VMEM((3, 2 * half, 9 * width), bf16),
            pltpu.VMEM((9, 2 * low_cols, 9 * width), bf16),
            pltpu.VMEM((6, fine_cols + 16, width), f32),
            pltpu.VMEM((chips, frames, low_cols, 2 * half), f32),
            pltpu.VMEM((chips, frames - 1, low_cols, 2 * half), f32),
            pltpu.VMEM((low_cols, channels), f32),
            pltpu.VMEM((low_cols, channels), f32),
            pltpu.VMEM((8, channels), f32),
            pltpu.VMEM((channels, channels), bf16),
            pltpu.VMEM((2, frames * count, channels // 64, 128), f32),
            dma((5,)),
            dma((frames - 1,)),
            dma((frames - 1,)),
            dma((2,)),
            dma((2,)),
            dma((2, chips - 1, 3)),
            dma((2, chips - 1, 3)),
            dma((chips, 3)),
            dma((chips, 3)),
            dma((chips, frames - 1)),
            dma((chips, frames - 1)),
            dma((2, frames * count - 1)),
            dma((2, frames * count - 1)),
        ],
        compiler_params=pltpu.CompilerParams(
            collective_id=0, has_side_effects=True, vmem_limit_bytes=60 * 1024 * 1024
        ),
        cost_estimate=pl.CostEstimate(
            flops=2 * products, bytes_accessed=2 * 1024 * 1024, transcendentals=low_cols * channels
        ),
    )(
        cotangent.reshape(cotangent.shape[1:]),
        conv_weight.reshape((27, half, width)),
        latent.reshape((low_cols, channels)),
        norm_gain.reshape((1, channels)),
        norm_bias.reshape((1, channels)),
    )
    return grad.reshape(latent.shape), sums[1], sums[0]


def on_device(latent, norm_gain, norm_bias, conv_weight, cotangent):
    half, width = conv_weight.shape[3:]
    per_group = latent.shape[3] // GROUPS
    fits = (
        lax.axis_size("tm") == 4
        and latent.shape[1] == 1
        and latent.shape[3] % 512 == 0
        and lax.axis_size("rows") % 2 == 0
        and half % 64 == 0
        and width % 128 == 0
        and latent.shape[2] % 16 == 0
        and per_group & (per_group - 1) == 0
    )
    run = fused if fits else spread_out
    return run(latent, norm_gain, norm_bias, conv_weight, cotangent)


def solution(mesh):
    placed = (
        P("tm", "rows", None, None),
        P(),
        P(),
        P(None, None, None, "rows", "tm"),
        P("tm", "rows", None, None),
    )
    return jax.shard_map(
        on_device,
        mesh=mesh,
        in_specs=placed,
        out_specs=(P("tm", "rows", None, None), P(), P()),
        check_vma=False,
    )
```
